256 devices in a mesh: row: 64 (over z, x, core), col: 4 (over y).
Axes of the slice: x: 4, y: 4, z: 8, core: 2. Of those that a mesh axis runs over, the one named last changes fastest.
Arguments:
- new_embeddings: bfloat16 [32768, 1024], P('row'), may hold values from -6 to 6, as said below
- old_vectors: bfloat16 [16384, 1024], P(('col', 'row')), may hold values from -6 to 6, as said below
Outputs:
- gradient: float32 [32768, 1024], P('row', 'col')
- loss: float32 [], replicated
The draws below stay inside these ranges and needn't reach their ends.
Inputs may be any that keep to these rules, and one draw needn't show every extreme that they name: `new_embeddings`: entries of order one. `old_vectors`: entries of order one.
All inputs are finite; a program needn't handle non-finite values.
Results may differ from the reference program's by a relative error of at most 0.0017.
Values may be sent and summed in bfloat16 or wider, within the bound.
A program may use at most 64 MiB of HBM per device.

```python
import math
import jax
import jax.numpy as jnp
from jax import lax

D = 1024
ITERS = 3
NEW_TOTAL = 32768
OLD_TOTAL = 16384


def shared_old(key):
    return jax.random.normal(key, (OLD_TOTAL, D), jnp.float32)


def draw_old_vectors(key, part):
    base = shared_old(key)
    return jnp.clip(base, -6.0, 6.0).astype(jnp.bfloat16)


def draw_new_embeddings(key, part):
    key = jax.random.fold_in(key, 23)
    fresh = jax.random.normal(key, (NEW_TOTAL, D), jnp.float32)
    return jnp.clip(fresh, -6.0, 6.0).astype(jnp.bfloat16)


def setup_inputs(seed: int = 0) -> dict:
    key_list = jax.random.split(jax.random.key(seed), 3)
    new_embeddings = draw_new_embeddings(jax.random.fold_in(key_list[2], 71), 0)
    old_vectors = draw_old_vectors(jax.random.fold_in(key_list[2], 71), 0)
    return dict(new_embeddings=new_embeddings, old_vectors=old_vectors)


EPSILON = 0.01


def cost_block(block, old, old_norms):
    row_norms = jnp.sum(jnp.square(block.astype(jnp.float32)), axis=1)
    inner = lax.dot_general(block, old, (((1,), (1,)), ((), ())), preferred_element_type=jnp.float32)
    return (row_norms[:, None] + old_norms[None, :] - 2.0 * inner) / D


def reference(new_embeddings, old_vectors):
    width = math.gcd(NEW_TOTAL, 512)
    blocks = new_embeddings.reshape(NEW_TOTAL // width, width, D)
    old_norms = jnp.sum(jnp.square(old_vectors.astype(jnp.float32)), axis=1)
    cost_all = lax.map(lambda block: cost_block(block, old_vectors, old_norms), blocks)
    col_pot = jnp.zeros((OLD_TOTAL,), jnp.float32)

    def column_step(carry, pair):
        tile, pots = pair
        scaled = (pots[:, None] - tile) / EPSILON
        top = jnp.max(scaled, axis=0)
        total = jnp.sum(jnp.exp(scaled - top[None, :]), axis=0)
        best = jnp.maximum(carry[0], top)
        return (best, carry[1] * jnp.exp(carry[0] - best) + total * jnp.exp(top - best)), None

    for sweep in range(ITERS):
        row_pot = lax.map(lambda tile: -EPSILON * math.log(OLD_TOTAL) - EPSILON * jax.nn.logsumexp((col_pot[None, :] - tile) / EPSILON, axis=1), cost_all)
        start = (jnp.full((OLD_TOTAL,), -jnp.inf, jnp.float32), jnp.zeros((OLD_TOTAL,), jnp.float32))
        (col_top, col_sum), unused = lax.scan(column_step, start, (cost_all, row_pot))
        col_pot = -EPSILON * math.log(NEW_TOTAL) - EPSILON * (col_top + jnp.log(col_sum))

    def finish(triple):
        tile, pots, block = triple
        plan = jnp.exp((pots[:, None] + col_pot[None, :] - tile) / EPSILON)
        part = jnp.sum(plan * tile)
        mass = jnp.sum(plan, axis=1)
        moved = jnp.dot(plan.astype(jnp.bfloat16), old_vectors, preferred_element_type=jnp.float32)
        return part, NEW_TOTAL * (block.astype(jnp.float32) * mass[:, None] - moved)

    parts, gradient = lax.map(finish, (cost_all, row_pot, blocks))
    return gradient.reshape(NEW_TOTAL, D), jnp.sum(parts)
```

```python
import math

import jax
import jax.numpy as jnp
from jax import lax
from jax.experimental import pallas as pl
from jax.experimental.pallas import tpu as pltpu
from jax.sharding import PartitionSpec as P

MESH = pl.DeviceIdType.MESH
EPSILON = 0.01
RATE = math.log2(math.e) / EPSILON
LIFT = 40.0

NX, NCORE, NY = 4, 2, 4
SUB = 32


def body_kernel(
    x_hbm, y_hbm, g_ref, loss_ref,
    xc, yg, cost, ex, plan_low, xn, top, tot, rowb, yn, vcol, tcol,
    rs1, rr1, rs2, rr2,
    cxs1, cxr1, czs1, czr1, cxs2, cxr2, czs2, czr2,
    lzs, lzr, lxs, lxr, lys, lyr,
    half_out, half_own, half_in, part_out, part_in,
    local_sem, xcore_sem, gsend, ax_sem, az_sem, bz_sem, bx_sem,
    ex_send, ex_recv, hs_sem, hr_sem, ps_sem, pr_sem,
):
    rows, depth = x_hbm.shape
    shard = y_hbm.shape[0]
    nrow, ncol = cost.shape
    nz = lax.axis_size("row") // (NX * NCORE)
    r = lax.axis_index("row")
    y = lax.axis_index("col")
    z = r // (NX * NCORE)
    x = (r // NCORE) % NX
    c = r % NCORE
    new_total = rows * lax.axis_size("row")
    old_total = shard * lax.axis_size("row") * lax.axis_size("col")
    lanes_a = 3 * depth // 8
    reach = nz // 2

    def dev(dz=0, dx=0, dc=0, dy=0):
        zz = lax.rem(z + dz + nz, nz)
        xx = lax.rem(x + dx + NX, NX)
        cc = lax.rem(c + dc, NCORE)
        yy = lax.rem(y + dy + NY, NY)
        return ((zz * NX + xx) * NCORE + cc, yy)

    z_peers = [dev(dz=d) for d in range(1, nz)]
    x_peers = [dev(dx=d) for d in range(1, NX)]
    y_peers = [dev(dy=d, dc=e) for d in range(NY) for e in range(NCORE) if d or e]

    barrier = pltpu.get_barrier_semaphore()
    everyone = z_peers + x_peers + y_peers
    for p in everyone:
        pl.semaphore_signal(barrier, inc=1, device_id=p, device_id_type=MESH)
    pl.semaphore_wait(barrier, len(everyone))

    part_lanes = {"a": pl.ds(0, lanes_a), "b": pl.ds(lanes_a, depth - lanes_a)}

    def region(dz, dx, part, half=None):
        slot = lax.rem(z + dz + nz, nz) * NX + lax.rem(x + dx + NX, NX)
        first = 0 if half is None else half * (shard // 2)
        count = shard if half is None else shard // 2
        start = pl.multiple_of(slot * shard + first, shard // 2)
        return yg.at[pl.ds(start, count), part_lanes[part]]

    def send(part, dst, sem, target, half=None, own=False):
        src = dst
        if own:
            src = y_hbm.at[:, part_lanes[part]]
        pltpu.make_async_remote_copy(
            src, dst, gsend.at[0 if part == "a" else 1], sem, device_id=target, device_id_type=MESH
        ).start()

    def arrived(ref, sem):
        pltpu.make_async_copy(ref, ref, sem).wait()

    zstep = (dev(dz=1), dev(dz=-1))
    xstep = (dev(dx=1), dev(dx=-1))
    xi_of = (0, -1, 1, 2)
    order_dz = [0] + [s * d for d in range(1, reach) for s in (-1, 1)] + [reach]
    place = {dz: i for i, dz in enumerate(order_dz)}

    def send_bx(dz, own=False):
        for way in (0, 1):
            send("b", region(dz, 0, "b"), bx_sem.at[place[dz], way], xstep[way], own=own)

    def send_az(xi, own=False):
        for way in (0, 1):
            send("a", region(0, xi_of[xi], "a"), az_sem.at[way, 0, xi], zstep[way], own=own)

    def on_ax(k):
        if k < 2:
            dx = -1 if k == 0 else 1
            arrived(region(0, dx, "a"), ax_sem.at[k])
            send("a", region(0, dx, "a", k), ax_sem.at[2 + k], xstep[k])
            send_az(1 + k)
        else:
            arrived(region(0, -2 if k == 2 else 2, "a", k - 2), ax_sem.at[k])
            if k == 3:
                send_az(3)

    def on_ring(part, way, d, dx, sems):
        sign = -1 if way == 0 else 1
        if d < reach:
            arrived(region(sign * d, dx, part), sems(d - 1))
            if d < reach - 1:
                send(part, region(sign * d, dx, part), sems(d), zstep[way])
            else:
                send(part, region(sign * d, dx, part, way), sems(d), zstep[way])
        else:
            arrived(region(sign * d, dx, part, way), sems(d - 1))

    def on_az(d, xi):
        for way in (0, 1):
            on_ring("a", way, d, xi_of[xi], lambda i: az_sem.at[way, i, xi])

    def on_bz(d):
        for way in (0, 1):
            on_ring("b", way, d, 0, lambda i: bz_sem.at[way, i])
            if d < reach:
                send_bx(-d if way == 0 else d)
        if d == reach:
            send_bx(reach)

    def on_bx(dz, k):
        i = place[dz]
        if k < 2:
            dx = -1 if k == 0 else 1
            arrived(region(dz, dx, "b"), bx_sem.at[i, k])
            send("b", region(dz, dx, "b", k), bx_sem.at[i, 2 + k], xstep[k])
        else:
            arrived(region(dz, -2 if k == 2 else 2, "b", k - 2), bx_sem.at[i, k])

    own_slot = pl.ds(pl.multiple_of((z * NX + x) * shard, shard), shard)
    own_rows = pl.ds(pl.multiple_of(c * rows, rows), rows)
    other_rows = pl.ds(pl.multiple_of((1 - c) * rows, rows), rows)

    for way in (0, 1):
        send("b", region(0, 0, "b"), bz_sem.at[way, 0], zstep[way], own=True)
        send("a", region(0, 0, "a"), ax_sem.at[way], xstep[way], own=True)
    send_az(0, own=True)
    send_bx(0, own=True)
    x_copy = pltpu.make_async_remote_copy(
        x_hbm, xc.at[own_rows], xcore_sem.at[0], xcore_sem.at[1], device_id=dev(dc=1), device_id_type=MESH
    )
    x_copy.start()
    x_local = pltpu.make_async_copy(x_hbm, xc.at[own_rows], local_sem.at[0])
    y_local = pltpu.make_async_copy(y_hbm, yg.at[own_slot], local_sem.at[1])
    x_local.start()
    y_local.start()

    top[...] = jnp.full(top.shape, 1e30, jnp.float32)
    tot[...] = jnp.zeros(tot.shape, jnp.float32)

    def row_norms(half):
        def step(i, carry):
            rs = pl.ds(pl.multiple_of(half * rows + i * SUB, SUB), SUB)
            v = jnp.square(xc[rs, :].astype(jnp.float32))
            xn[rs, :] = jnp.broadcast_to(jnp.sum(v, axis=1, keepdims=True), (SUB, 128))
            return carry

        lax.fori_loop(0, rows // SUB, step, 0)

    group = NX * shard
    tile = 256

    def compute(dz):
        col0 = pl.multiple_of(lax.rem(z + dz + nz, nz) * group, group)
        cols = pl.ds(col0, group)
        sq = jnp.square(yg[cols, :].astype(jnp.float32))
        high = sq.astype(jnp.bfloat16)
        low = (sq - high.astype(jnp.float32)).astype(jnp.bfloat16)
        ones = jnp.ones((16, depth), jnp.bfloat16)
        nt = (((1,), (1,)), ((), ()))
        norms = lax.dot_general(ones, high, nt, preferred_element_type=jnp.float32)
        norms = norms + lax.dot_general(ones, low, nt, preferred_element_type=jnp.float32)
        yn[:, cols] = norms[0:1, :]

        def step(i, carry):
            r0 = pl.multiple_of(i * tile, tile)
            rs = pl.ds(r0, tile)
            inner = lax.dot_general(xc[rs, :], yg[cols, :], nt, preferred_element_type=jnp.float32)
            best = top[rs, :]
            parts = []
            xrow = xn[rs, :]
            for b in range(group // 128):
                cs = pl.ds(pl.multiple_of(col0 + b * 128, 128), 128)
                val = (xrow + yn[:, cs] - 2.0 * inner[:, b * 128 : (b + 1) * 128]) * (1.0 / depth)
                cost[rs, cs] = val
                parts.append(val)
            low_ = best
            for val in parts:
                low_ = jnp.minimum(low_, val)
            acc = tot[rs, :] * jnp.exp2((low_ - best) * RATE)
            for val in parts:
                acc = acc + jnp.exp2((low_ - val) * RATE)
            top[rs, :] = low_
            tot[rs, :] = acc
            return carry

        lax.fori_loop(0, nrow // tile, step, 0)

    on_ax(0)
    on_ax(1)
    on_bz(1)
    on_az(1, 0)
    on_bx(0, 0)
    on_bx(0, 1)
    on_ax(2)
    on_ax(3)
    on_az(1, 1)
    on_az(1, 2)
    x_local.wait()
    y_local.wait()
    x_copy.wait()
    row_norms(0)
    row_norms(1)
    on_bx(0, 2)
    on_bx(0, 3)
    on_az(1, 3)
    on_bz(2)
    compute(0)
    for k in (0, 1):
        on_bx(-1, k)
        on_bx(1, k)
    for xi in range(4):
        on_az(2, xi)
    for k in (2, 3):
        on_bx(-1, k)
        on_bx(1, k)
    on_bz(3)
    compute(-1)
    for k in (0, 1):
        on_bx(-2, k)
        on_bx(2, k)
    compute(1)
    for xi in range(4):
        on_az(3, xi)
    on_bz(4)
    for k in (2, 3):
        on_bx(-2, k)
        on_bx(2, k)
    for k in (0, 1):
        on_bx(-3, k)
        on_bx(3, k)
    compute(-2)
    for k in (0, 1):
        on_bx(4, k)
    compute(2)
    for k in (2, 3):
        on_bx(-3, k)
        on_bx(3, k)
    compute(-3)
    compute(3)
    for xi in range(4):
        on_az(4, xi)
    for k in (2, 3):
        on_bx(4, k)
    compute(4)

    def start(send_ref, recv_ref, i, peers):
        for j, p in enumerate(peers):
            pltpu.make_async_remote_copy(
                send_ref, recv_ref.at[j], ex_send.at[i], ex_recv.at[i], device_id=p, device_id_type=MESH
            ).start()

    def finish(recv_ref, i):
        pltpu.make_async_copy(recv_ref, recv_ref, ex_recv.at[i]).wait()
        pltpu.make_async_copy(recv_ref, recv_ref, ex_send.at[i]).wait()

    def to_rows(line):
        return jnp.transpose(jnp.broadcast_to(line, (128, nrow)))

    top_t = jnp.transpose(top[...])
    tot_t = jnp.transpose(tot[...])
    low = jnp.min(top_t, axis=0, keepdims=True)
    mass = jnp.sum(tot_t * jnp.exp2((low - top_t) * RATE), axis=0, keepdims=True)
    rs1[:, 0:nrow] = low
    rs1[:, nrow : 2 * nrow] = mass
    start(rs1, rr1, 0, y_peers)
    finish(rr1, 0)
    lows = [low] + [rr1[j, :, 0:nrow] for j in range(len(y_peers))]
    masses = [mass] + [rr1[j, :, nrow : 2 * nrow] for j in range(len(y_peers))]
    low = lows[0]
    for v in lows[1:]:
        low = jnp.minimum(low, v)
    mass = sum(m * jnp.exp2((low - v) * RATE) for v, m in zip(lows, masses))
    rowb[...] = to_rows(low * RATE - jnp.log2(mass) - math.log2(old_total))

    nb = ncol // 128

    def fold(v, join):
        out = v[0:8]
        for i in range(1, v.shape[0] // 8):
            out = join(out, v[8 * i : 8 * i + 8])
        return out

    def highest(i, carry):
        rs = pl.ds(pl.multiple_of(i * SUB, SUB), SUB)
        rb = rowb[rs, :]
        out = []
        for b in range(nb):
            cs = pl.ds(b * 128, 128)
            a = rb - cost[rs, cs] * RATE
            ex[rs, cs] = a
            out.append(jnp.maximum(carry[b], fold(a, jnp.maximum)))
        return tuple(out)

    carry = lax.fori_loop(
        0, nrow // SUB, highest, tuple(jnp.full((8, 128), -3e38, jnp.float32) for _ in range(nb))
    )
    for b in range(nb):
        tcol[:, b * 128 : (b + 1) * 128] = jnp.max(carry[b], axis=0, keepdims=True)

    def scaled(i, carry):
        rs = pl.ds(pl.multiple_of(i * SUB, SUB), SUB)
        out = []
        for b in range(nb):
            cs = pl.ds(b * 128, 128)
            e = jnp.exp2(ex[rs, cs] - (tcol[:, cs] - LIFT))
            ex[rs, cs] = e
            out.append(carry[b] + fold(e, jnp.add))
        return tuple(out)

    zeros = tuple(jnp.zeros((8, 128), jnp.float32) for _ in range(nb))
    carry = lax.fori_loop(0, nrow // SUB, scaled, zeros)
    cxs1[:, 0:ncol] = tcol[...]
    for b in range(nb):
        cxs1[:, ncol + b * 128 : ncol + (b + 1) * 128] = jnp.sum(carry[b], axis=0, keepdims=True)

    def merge(own, recv, n):
        tops = [own[:, 0:ncol]] + [recv[j, :, 0:ncol] for j in range(n)]
        sums = [own[:, ncol:]] + [recv[j, :, ncol:] for j in range(n)]
        best = tops[0]
        for v in tops[1:]:
            best = jnp.maximum(best, v)
        return best, sum(s * jnp.exp2(v - best) for v, s in zip(tops, sums))

    start(cxs1, cxr1, 1, x_peers)
    finish(cxr1, 1)
    best, total = merge(cxs1[...], cxr1, len(x_peers))
    czs1[:, 0:ncol] = best
    czs1[:, ncol:] = total
    start(czs1, czr1, 2, z_peers)
    finish(czr1, 2)
    best, total = merge(czs1[...], czr1, len(z_peers))
    grow = 2.0 ** (2 * LIFT) / new_total
    vcol[...] = jnp.exp2(tcol[...] - best) * grow / total

    for sweep in range(2):
        def row_sums(i, carry):
            rs = pl.ds(pl.multiple_of(i * SUB, SUB), SUB)
            acc = ex[rs, 0:128] * vcol[:, 0:128]
            for b in range(1, nb):
                cs = pl.ds(b * 128, 128)
                acc = acc + ex[rs, cs] * vcol[:, cs]
            tot[rs, :] = acc
            return carry

        lax.fori_loop(0, nrow // SUB, row_sums, 0)
        line = jnp.sum(jnp.transpose(tot[...]), axis=0, keepdims=True)
        i = 3 + 3 * sweep
        rs2[sweep] = line
        start(rs2.at[sweep], rr2.at[sweep], i, y_peers)
        finish(rr2.at[sweep], i)
        line = line + sum(rr2[sweep, j] for j in range(len(y_peers)))
        rowb[...] = to_rows((2.0 ** (2 * LIFT) / old_total) / line)

        def col_sums(i, carry):
            rs = pl.ds(pl.multiple_of(i * SUB, SUB), SUB)
            rb = rowb[rs, :]
            return tuple(
                carry[b] + fold(ex[rs, pl.ds(b * 128, 128)] * rb, jnp.add) for b in range(nb)
            )

        carry = lax.fori_loop(0, nrow // SUB, col_sums, zeros)
        for b in range(nb):
            cs = pl.ds(b * 128, 128)
            cxs2[sweep, :, cs] = vcol[:, cs] * jnp.sum(carry[b], axis=0, keepdims=True)
        start(cxs2.at[sweep], cxr2.at[sweep], i + 1, x_peers)
        finish(cxr2.at[sweep], i + 1)
        czs2[sweep] = cxs2[sweep] + sum(cxr2[sweep, j] for j in range(len(x_peers)))
        start(czs2.at[sweep], czr2.at[sweep], i + 2, z_peers)
        finish(czr2.at[sweep], i + 2)
        total = czs2[sweep] + sum(czr2[sweep, j] for j in range(len(z_peers)))
        vcol[...] = vcol[...] * (grow / total)

    def planned(i, carry):
        rs = pl.ds(pl.multiple_of(i * SUB, SUB), SUB)
        rb = rowb[rs, :] * 2.0 ** (-2 * LIFT)
        mass = jnp.zeros((SUB, 128), jnp.float32)
        part = jnp.zeros((SUB, 128), jnp.float32)
        for b in range(nb):
            cs = pl.ds(b * 128, 128)
            p = ex[rs, cs] * rb * vcol[:, cs]
            plan_low[rs, cs] = p.astype(jnp.bfloat16)
            mass = mass + p
            part = part + p * cost[rs, cs]
        tot[rs, :] = jnp.broadcast_to(jnp.sum(mass, axis=1, keepdims=True), (SUB, 128))
        return carry + fold(part, jnp.add)

    part = lax.fori_loop(0, nrow // SUB, planned, jnp.zeros((8, 128), jnp.float32))
    lzs[...] = jnp.sum(part, axis=0, keepdims=True)
    start(lzs, lzr, 9, z_peers)

    width = g_ref.shape[1]
    turn = (2, 1, 3, 0)
    y_target = {d: dev(dy=d) for d in (1, 2, 3)}

    def product(ci):
        q = lax.rem(y + turn[ci], NY)
        lanes = pl.ds(pl.multiple_of(q * width, width), width)
        for which, out in ((other_rows, half_out), (own_rows, half_own)):
            base = (1 - c) * rows if out is half_out else c * rows

            def step(i, carry):
                rs = pl.ds(pl.multiple_of(base + i * tile, tile), tile)
                moved = jnp.dot(plan_low[rs, :], yg[:, lanes], preferred_element_type=jnp.float32)
                m = tot[rs, :]
                xs = xc[rs, lanes].astype(jnp.float32)
                os = pl.ds(pl.multiple_of(i * tile, tile), tile)
                for b in range(width // 128):
                    cs = slice(b * 128, (b + 1) * 128)
                    out[ci, os, cs] = xs[:, cs] * m - moved[:, cs]
                return carry

            lax.fori_loop(0, rows // tile, step, 0)
            if out is half_out:
                half_copy(ci).start()

    def half_copy(ci):
        return pltpu.make_async_remote_copy(
            half_out.at[ci], half_in.at[ci], hs_sem.at[ci], hr_sem.at[ci],
            device_id=dev(dc=1), device_id_type=MESH,
        )

    def part_copy(ci):
        return pltpu.make_async_remote_copy(
            part_out.at[ci], part_in.at[ci], ps_sem.at[ci], pr_sem.at[ci],
            device_id=y_target[turn[ci]], device_id_type=MESH,
        )

    def pass_on(ci):
        half_copy(ci).wait()
        part_out[ci] = (half_own[ci] + half_in[ci]).astype(jnp.bfloat16)
        part_copy(ci).start()

    product(0)
    product(1)
    pass_on(0)
    finish(lzr, 9)
    lxs[...] = lzs[...] + sum(lzr[j] for j in range(len(z_peers)))
    start(lxs, lxr, 10, x_peers)
    product(2)
    pass_on(1)
    product(3)
    pass_on(2)
    finish(lxr, 10)
    lys[...] = lxs[...] + sum(lxr[j] for j in range(len(x_peers)))
    start(lys, lyr, 11, y_peers)
    half_copy(3).wait()
    half_own[3] = half_own[3] + half_in[3]
    finish(lyr, 11)
    loss = lys[...] + sum(lyr[j] for j in range(len(y_peers)))
    loss_ref[...] = jnp.broadcast_to(jnp.sum(loss, axis=1, keepdims=True), loss_ref.shape)
    for ci in (0, 1, 2):
        part_copy(ci).wait()
    g_ref[...] = float(new_total) * (
        half_own[3] + part_in[0].astype(jnp.float32) + part_in[1].astype(jnp.float32) + part_in[2].astype(jnp.float32)
    )
    others = (nz * NX - 1) * shard
    for i, part in ((0, "a"), (1, "b")):
        sent = yg.at[pl.ds(0, others), part_lanes[part]]
        pltpu.make_async_copy(sent, sent, gsend.at[i]).wait()


def solution(mesh):
    def body(new_embeddings, old_vectors):
        rows, depth = new_embeddings.shape
        shard = old_vectors.shape[0]
        nz = lax.axis_size("row") // (NX * NCORE)
        nrow, ncol = rows * NCORE, shard * nz * NX
        width = depth // NY
        f32, bf16 = jnp.float32, jnp.bfloat16
        ny, npx, npz = NY * NCORE - 1, NX - 1, nz - 1
        dma = pltpu.SemaphoreType.DMA
        scratch = [
            pltpu.VMEM((nrow, depth), bf16),
            pltpu.VMEM((ncol, depth), bf16),
            pltpu.VMEM((nrow, ncol), f32),
            pltpu.VMEM((nrow, ncol), f32),
            pltpu.VMEM((nrow, ncol), bf16),
            pltpu.VMEM((nrow, 128), f32),
            pltpu.VMEM((nrow, 128), f32),
            pltpu.VMEM((nrow, 128), f32),
            pltpu.VMEM((nrow, 128), f32),
            pltpu.VMEM((1, ncol), f32),
            pltpu.VMEM((1, ncol), f32),
            pltpu.VMEM((1, ncol), f32),
            pltpu.VMEM((1, 2 * nrow), f32),
            pltpu.VMEM((ny, 1, 2 * nrow), f32),
            pltpu.VMEM((2, 1, nrow), f32),
            pltpu.VMEM((2, ny, 1, nrow), f32),
            pltpu.VMEM((1, 2 * ncol), f32),
            pltpu.VMEM((npx, 1, 2 * ncol), f32),
            pltpu.VMEM((1, 2 * ncol), f32),
            pltpu.VMEM((npz, 1, 2 * ncol), f32),
            pltpu.VMEM((2, 1, ncol), f32),
            pltpu.VMEM((2, npx, 1, ncol), f32),
            pltpu.VMEM((2, 1, ncol), f32),
            pltpu.VMEM((2, npz, 1, ncol), f32),
            pltpu.VMEM((1, 128), f32),
            pltpu.VMEM((npz, 1, 128), f32),
            pltpu.VMEM((1, 128), f32),
            pltpu.VMEM((npx, 1, 128), f32),
            pltpu.VMEM((1, 128), f32),
            pltpu.VMEM((ny, 1, 128), f32),
            pltpu.VMEM((4, rows, width), f32),
            pltpu.VMEM((4, rows, width), f32),
            pltpu.VMEM((4, rows, width), f32),
            pltpu.VMEM((3, rows, width), bf16),
            pltpu.VMEM((3, rows, width), bf16),
            dma((2,)),
            dma((2,)),
            dma((2,)),
            dma((4,)),
            dma((2, nz // 2, 4)),
            dma((2, nz // 2)),
            dma((nz, 4)),
            dma((12,)),
            dma((12,)),
            dma((4,)),
            dma((4,)),
            dma((3,)),
            dma((3,)),
        ]
        gradient, loss = pl.pallas_call(
            body_kernel,
            out_shape=(
                jax.ShapeDtypeStruct((rows, width), f32),
                jax.ShapeDtypeStruct((1, 128), f32),
            ),
            in_specs=[pl.BlockSpec(memory_space=pl.ANY)] * 2,
            out_specs=[pl.BlockSpec(memory_space=pltpu.VMEM)] * 2,
            scratch_shapes=scratch,
            compiler_params=pltpu.CompilerParams(
                collective_id=0, has_side_effects=True, vmem_limit_bytes=56 << 20
            ),
            name="sinkhorn",
        )(new_embeddings, old_vectors)
        return gradient, loss[0, 0]

    placed = (P("row", None), P(("col", "row"), None))
    return jax.shard_map(
        body, mesh=mesh, in_specs=placed, out_specs=(P("row", "col"), P()), check_vma=False
    )
```

```python
import math

import jax
import jax.numpy as jnp
from jax import lax
from jax.experimental import pallas as pl
from jax.experimental.pallas import tpu as pltpu
from jax.sharding import PartitionSpec as P

MESH = pl.DeviceIdType.MESH
EPSILON = 0.01
RATE = 2.0 * math.log2(math.e) / EPSILON
LIFT = 40.0

NX, NCORE, NY = 4, 2, 4
SUB = 32


def body_kernel(
    x_hbm, y_hbm, g_ref, loss_ref,
    xc, yg, aff, ex, plan_low, xn, top, tot, rowb, vcol, tcol,
    rs1, rr1, rs2, rr2,
    cxs1, cxr1, czs1, czr1, cxs2, cxr2, czs2, czr2,
    lzs, lzr, lxs, lxr, lys, lyr,
    term, half_in, part_out, part_in,
    local_sem, xcore_sem, gsend, ax_sem, az_sem, bz_sem, bx_sem,
    ex_send, ex_recv, hs_sem, hr_sem, ps_sem, pr_sem,
):
    rows, depth = x_hbm.shape
    shard = y_hbm.shape[0]
    nrow, ncol = aff.shape
    rate = RATE / depth
    nz = lax.axis_size("row") // (NX * NCORE)
    r = lax.axis_index("row")
    y = lax.axis_index("col")
    z = r // (NX * NCORE)
    x = (r // NCORE) % NX
    c = r % NCORE
    new_total = rows * lax.axis_size("row")
    old_total = shard * lax.axis_size("row") * lax.axis_size("col")
    lanes_a = 3 * depth // 8
    reach = nz // 2

    def dev(dz=0, dx=0, dc=0, dy=0):
        zz = lax.rem(z + dz + nz, nz)
        xx = lax.rem(x + dx + NX, NX)
        cc = lax.rem(c + dc, NCORE)
        yy = lax.rem(y + dy + NY, NY)
        return ((zz * NX + xx) * NCORE + cc, yy)

    z_peers = [dev(dz=d) for d in range(1, nz)]
    x_peers = [dev(dx=d) for d in range(1, NX)]
    y_peers = [dev(dy=d, dc=e) for d in range(NY) for e in range(NCORE) if d or e]

    barrier = pltpu.get_barrier_semaphore()
    everyone = z_peers + x_peers + y_peers
    for p in everyone:
        pl.semaphore_signal(barrier, inc=1, device_id=p, device_id_type=MESH)
    pl.semaphore_wait(barrier, len(everyone))

    part_lanes = {"a": pl.ds(0, lanes_a), "b": pl.ds(lanes_a, depth - lanes_a)}

    def region(dz, dx, part, half=None):
        slot = lax.rem(z + dz + nz, nz) * NX + lax.rem(x + dx + NX, NX)
        first = 0 if half is None else half * (shard // 2)
        count = shard if half is None else shard // 2
        start = pl.multiple_of(slot * shard + first, shard // 2)
        return yg.at[pl.ds(start, count), part_lanes[part]]

    def send(part, dst, sem, target, half=None, own=False):
        src = dst
        if own:
            src = y_hbm.at[:, part_lanes[part]]
        pltpu.make_async_remote_copy(
            src, dst, gsend.at[0 if part == "a" else 1], sem, device_id=target, device_id_type=MESH
        ).start()

    def arrived(ref, sem):
        pltpu.make_async_copy(ref, ref, sem).wait()

    zstep = (dev(dz=1), dev(dz=-1))
    zjump = (dev(dz=2), dev(dz=-2))
    xstep = (dev(dx=1), dev(dx=-1))
    xi_of = (0, -1, 1, 2)
    order_dz = [0] + [s * d for d in range(1, reach) for s in (-1, 1)] + [reach]
    place = {dz: i for i, dz in enumerate(order_dz)}

    def send_bx(dz, own=False):
        for way in (0, 1):
            send("b", region(dz, 0, "b"), bx_sem.at[place[dz], way], xstep[way], own=own)

    def send_az(xi, own=False):
        for way in (0, 1):
            send("a", region(0, xi_of[xi], "a"), az_sem.at[way, 0, xi], zstep[way], own=own)

    def on_ax(k):
        arrived(region(0, (-1, 1, 2)[k], "a"), ax_sem.at[k])
        send_az(1 + k)

    def on_az(way, d, xi):
        sign = -1 if way == 0 else 1
        here = region(sign * d, xi_of[xi], "a", None if d < reach else way)
        arrived(here, az_sem.at[way, d - 1, xi])
        if d < reach:
            half = None if d < reach - 1 else way
            send("a", region(sign * d, xi_of[xi], "a", half), az_sem.at[way, d, xi], zstep[way])

    def on_bz(way, d):
        sign = -1 if way == 0 else 1
        arrived(region(sign * d, 0, "b", None if d < reach else way), bz_sem.at[way, d - 1])
        if d == 2:
            send("b", region(sign * d, 0, "b"), bz_sem.at[way, 2], zstep[way])
            send("b", region(sign * d, 0, "b", way), bz_sem.at[way, 3], zjump[way])
        if d < reach:
            send_bx(sign * d)
        elif way == 1:
            send_bx(reach)

    def on_bx(dz, k):
        i = place[dz]
        if k < 2:
            dx = -1 if k == 0 else 1
            arrived(region(dz, dx, "b"), bx_sem.at[i, k])
            send("b", region(dz, dx, "b", k), bx_sem.at[i, 2 + k], xstep[k])
        else:
            arrived(region(dz, -2 if k == 2 else 2, "b", k - 2), bx_sem.at[i, k])

    own_slot = pl.ds(pl.multiple_of((z * NX + x) * shard, shard), shard)
    own_rows = pl.ds(pl.multiple_of(c * rows, rows), rows)
    other_rows = pl.ds(pl.multiple_of((1 - c) * rows, rows), rows)

    for way in (0, 1):
        send("b", region(0, 0, "b"), bz_sem.at[way, 0], zstep[way], own=True)
    for way in (0, 1):
        send("b", region(0, 0, "b"), bz_sem.at[way, 1], zjump[way], own=True)
    for k, target in enumerate((*xstep, dev(dx=2))):
        send("a", region(0, 0, "a"), ax_sem.at[k], target, own=True)
    send_az(0, own=True)
    send_bx(0, own=True)
    x_copy = pltpu.make_async_remote_copy(
        x_hbm, xc.at[own_rows], xcore_sem.at[0], xcore_sem.at[1], device_id=dev(dc=1), device_id_type=MESH
    )
    x_copy.start()
    x_local = pltpu.make_async_copy(x_hbm, xc.at[own_rows], local_sem.at[0])
    y_local = pltpu.make_async_copy(y_hbm, yg.at[own_slot], local_sem.at[1])
    x_local.start()
    y_local.start()

    top[...] = jnp.full(top.shape, -1e30, jnp.float32)
    tot[...] = jnp.zeros(tot.shape, jnp.float32)

    group = NX * shard
    tile = 256

    def compute(dz):
        col0 = pl.multiple_of(lax.rem(z + dz + nz, nz) * group, group)
        cols = pl.ds(col0, group)
        block = yg[cols, :]
        sq = jnp.square(block.astype(jnp.float32))
        part = sq[:, 0:128]
        for b in range(1, depth // 128):
            part = part + sq[:, b * 128 : (b + 1) * 128]
        half_norm = 0.5 * jnp.sum(jnp.transpose(part), axis=0, keepdims=True)
        inner = lax.dot_general(
            xc[...], block, (((1,), (1,)), ((), ())), preferred_element_type=jnp.float32
        )
        aff[:, cols] = inner - half_norm

        def step(i, carry):
            rs = pl.ds(pl.multiple_of(i * tile, tile), tile)
            best = top[rs, :]
            parts = [
                aff[rs, pl.ds(pl.multiple_of(col0 + b * 128, 128), 128)] for b in range(group // 128)
            ]
            high = best
            for val in parts:
                high = jnp.maximum(high, val)
            acc = tot[rs, :] * jnp.exp2((best - high) * rate)
            for val in parts:
                acc = acc + jnp.exp2((val - high) * rate)
            top[rs, :] = high
            tot[rs, :] = acc
            return carry

        lax.fori_loop(0, nrow // tile, step, 0)

    schedule = (
        (on_ax, 0), (on_ax, 1), (on_bz, 0, 1), (on_bz, 1, 1), (on_ax, 2), (on_bx, 0, 0), (on_bx, 0, 1),
        (on_bz, 0, 2), (on_bz, 1, 2), (on_az, 0, 1, 0), (on_az, 1, 1, 0), (on_bx, -1, 0), (on_bx, -1, 1),
        (on_az, 0, 1, 1), (on_az, 1, 1, 1), (on_az, 0, 1, 2), (on_az, 1, 1, 2), (on_bx, 1, 0), (on_bx, 1, 1),
        (on_az, 0, 1, 3), (on_az, 1, 1, 3), (on_bx, 0, 2), (on_bx, 0, 3), (compute, 0), (on_bz, 0, 3),
        (on_bz, 1, 3), (on_bx, -2, 0), (on_bx, -2, 1), (on_bz, 0, 4), (on_bz, 1, 4), (on_bx, 2, 0),
        (on_bx, 2, 1), (on_bx, -1, 2), (on_bx, -1, 3), (compute, -1), (on_az, 0, 2, 0), (on_az, 1, 2, 0),
        (on_bx, 1, 2), (on_bx, 1, 3), (on_az, 0, 2, 1), (on_az, 1, 2, 1), (compute, 1), (on_az, 0, 2, 2),
        (on_az, 1, 2, 2), (on_bx, -3, 0), (on_bx, -3, 1), (on_az, 0, 2, 3), (on_az, 1, 2, 3), (on_bx, 3, 0),
        (on_bx, 3, 1), (on_bx, -2, 2), (on_bx, -2, 3), (compute, -2), (on_az, 0, 3, 0), (on_az, 1, 3, 0),
        (on_az, 0, 3, 1), (on_az, 1, 3, 1), (on_bx, 4, 0), (on_bx, 4, 1), (on_az, 0, 3, 2), (on_az, 1, 3, 2),
        (on_bx, 2, 2), (on_bx, 2, 3), (compute, 2), (on_bx, -3, 2), (on_bx, -3, 3), (on_az, 0, 3, 3),
        (on_az, 1, 3, 3), (compute, -3), (on_bx, 3, 2), (on_bx, 3, 3), (on_az, 0, 4, 0), (on_az, 1, 4, 0),
        (compute, 3), (on_az, 0, 4, 1), (on_az, 1, 4, 1), (on_bx, 4, 2), (on_bx, 4, 3), (on_az, 0, 4, 2),
        (on_az, 1, 4, 2), (on_az, 0, 4, 3), (on_az, 1, 4, 3), (compute, 4),
    )
    stages = [[]]
    for act, *where in schedule:
        if act is compute:
            stages.append([])
        else:
            stages[-1].append((act, where))

    def stage(i, carry):
        for k, events in enumerate(stages[:nz]):

            @pl.when(i == k)
            def _(k=k, events=events):
                for act, where in events:
                    act(*where)
                if k == 0:
                    x_local.wait()
                    y_local.wait()
                    x_copy.wait()

        far = (i + 1) // 2
        compute(far - 2 * far * (i % 2))
        return carry

    lax.fori_loop(0, nz, stage, 0)

    def start(send_ref, recv_ref, i, peers):
        for j, p in enumerate(peers):
            pltpu.make_async_remote_copy(
                send_ref, recv_ref.at[j], ex_send.at[i], ex_recv.at[i], device_id=p, device_id_type=MESH
            ).start()

    def finish(recv_ref, i):
        pltpu.make_async_copy(recv_ref, recv_ref, ex_recv.at[i]).wait()
        pltpu.make_async_copy(recv_ref, recv_ref, ex_send.at[i]).wait()

    def to_rows(line):
        return jnp.transpose(jnp.broadcast_to(line, (128, nrow)))

    top_t = jnp.transpose(top[...])
    tot_t = jnp.transpose(tot[...])
    high = jnp.max(top_t, axis=0, keepdims=True)
    mass = jnp.sum(tot_t * jnp.exp2((top_t - high) * rate), axis=0, keepdims=True)
    rs1[:, 0:nrow] = high
    rs1[:, nrow : 2 * nrow] = mass
    start(rs1, rr1, 0, y_peers)

    def row_norms(i, carry):
        rs = pl.ds(pl.multiple_of(i * tile, tile), tile)
        part = jnp.zeros((tile, 128), jnp.float32)
        for b in range(depth // 128):
            part = part + jnp.square(xc[rs, b * 128 : (b + 1) * 128].astype(jnp.float32))
        xn[rs, :] = jnp.broadcast_to(0.5 * jnp.sum(part, axis=1, keepdims=True), (tile, 128))
        return carry

    lax.fori_loop(0, nrow // tile, row_norms, 0)
    finish(rr1, 0)
    highs = [high] + [rr1[j, :, 0:nrow] for j in range(len(y_peers))]
    masses = [mass] + [rr1[j, :, nrow : 2 * nrow] for j in range(len(y_peers))]
    high = highs[0]
    for v in highs[1:]:
        high = jnp.maximum(high, v)
    mass = sum(m * jnp.exp2((v - high) * rate) for v, m in zip(highs, masses))
    rowb[...] = to_rows(-high - (jnp.log2(mass) + math.log2(old_total)) / rate)

    nb = ncol // 128

    def fold(v, join):
        out = v[0:8]
        for i in range(1, v.shape[0] // 8):
            out = join(out, v[8 * i : 8 * i + 8])
        return out

    def highest(i, carry):
        rs = pl.ds(pl.multiple_of(i * SUB, SUB), SUB)
        rb = rowb[rs, :]
        out = []
        for b in range(nb):
            cs = pl.ds(b * 128, 128)
            a = rb + aff[rs, cs]
            ex[rs, cs] = a
            out.append(jnp.maximum(carry[b], fold(a, jnp.maximum)))
        return tuple(out)

    carry = lax.fori_loop(
        0, nrow // SUB, highest, tuple(jnp.full((8, 128), -3e38, jnp.float32) for _ in range(nb))
    )
    for b in range(nb):
        tcol[:, b * 128 : (b + 1) * 128] = jnp.max(carry[b], axis=0, keepdims=True) - LIFT / rate

    def scaled(i, carry):
        rs = pl.ds(pl.multiple_of(i * SUB, SUB), SUB)
        out = []
        for b in range(nb):
            cs = pl.ds(b * 128, 128)
            e = jnp.exp2((ex[rs, cs] - tcol[:, cs]) * rate)
            ex[rs, cs] = e
            out.append(carry[b] + fold(e, jnp.add))
        return tuple(out)

    zeros = tuple(jnp.zeros((8, 128), jnp.float32) for _ in range(nb))
    carry = lax.fori_loop(0, nrow // SUB, scaled, zeros)
    cxs1[:, 0:ncol] = tcol[...]
    for b in range(nb):
        cxs1[:, ncol + b * 128 : ncol + (b + 1) * 128] = jnp.sum(carry[b], axis=0, keepdims=True)

    def merge(own, recv, n):
        tops = [own[:, 0:ncol]] + [recv[j, :, 0:ncol] for j in range(n)]
        sums = [own[:, ncol:]] + [recv[j, :, ncol:] for j in range(n)]
        best = tops[0]
        for v in tops[1:]:
            best = jnp.maximum(best, v)
        return best, sum(s * jnp.exp2((v - best) * rate) for v, s in zip(tops, sums))

    start(cxs1, cxr1, 1, x_peers)
    finish(cxr1, 1)
    best, total = merge(cxs1[...], cxr1, len(x_peers))
    czs1[:, 0:ncol] = best
    czs1[:, ncol:] = total
    start(czs1, czr1, 2, z_peers)
    finish(czr1, 2)
    best, total = merge(czs1[...], czr1, len(z_peers))
    grow = 2.0 ** (2 * LIFT) / new_total
    vcol[...] = jnp.exp2((tcol[...] - best) * rate) * grow / total

    def again(sweep, carry):
        def row_sums(i, carry):
            rs = pl.ds(pl.multiple_of(i * SUB, SUB), SUB)
            acc = ex[rs, 0:128] * vcol[:, 0:128]
            for b in range(1, nb):
                cs = pl.ds(b * 128, 128)
                acc = acc + ex[rs, cs] * vcol[:, cs]
            tot[rs, :] = acc
            return carry

        lax.fori_loop(0, nrow // SUB, row_sums, 0)
        line = jnp.sum(jnp.transpose(tot[...]), axis=0, keepdims=True)
        i = 3 + 3 * sweep
        rs2[sweep] = line
        start(rs2.at[sweep], rr2.at[sweep], i, y_peers)
        finish(rr2.at[sweep], i)
        line = line + sum(rr2[sweep, j] for j in range(len(y_peers)))
        rowb[...] = to_rows((2.0 ** (2 * LIFT) / old_total) / line)

        def col_sums(i, carry):
            rs = pl.ds(pl.multiple_of(i * SUB, SUB), SUB)
            rb = rowb[rs, :]
            return tuple(
                carry[b] + fold(ex[rs, pl.ds(b * 128, 128)] * rb, jnp.add) for b in range(nb)
            )

        sums = lax.fori_loop(0, nrow // SUB, col_sums, zeros)
        for b in range(nb):
            cs = pl.ds(b * 128, 128)
            cxs2[sweep, :, cs] = vcol[:, cs] * jnp.sum(sums[b], axis=0, keepdims=True)
        start(cxs2.at[sweep], cxr2.at[sweep], i + 1, x_peers)
        finish(cxr2.at[sweep], i + 1)
        czs2[sweep] = cxs2[sweep] + sum(cxr2[sweep, j] for j in range(len(x_peers)))
        start(czs2.at[sweep], czr2.at[sweep], i + 2, z_peers)
        finish(czr2.at[sweep], i + 2)
        total = czs2[sweep] + sum(czr2[sweep, j] for j in range(len(z_peers)))
        vcol[...] = vcol[...] * (grow / total)
        return carry

    lax.fori_loop(0, 2, again, 0)

    def planned(i, carry):
        rs = pl.ds(pl.multiple_of(i * SUB, SUB), SUB)
        rb = rowb[rs, :] * 2.0 ** (-2 * LIFT)
        xs = xn[rs, :]
        mass = jnp.zeros((SUB, 128), jnp.float32)
        part = jnp.zeros((SUB, 128), jnp.float32)
        for b in range(nb):
            cs = pl.ds(b * 128, 128)
            p = ex[rs, cs] * rb * vcol[:, cs]
            plan_low[rs, cs] = p.astype(jnp.bfloat16)
            mass = mass + p
            part = part + p * (xs - aff[rs, cs])
        tot[rs, :] = mass
        return carry + fold(part, jnp.add)

    part = lax.fori_loop(0, nrow // SUB, planned, jnp.zeros((8, 128), jnp.float32))
    lys[...] = jnp.sum(part, axis=0, keepdims=True)
    start(lys, lyr, 11, y_peers)

    def row_mass(i, carry):
        rs = pl.ds(pl.multiple_of(i * tile, tile), tile)
        tot[rs, :] = jnp.broadcast_to(jnp.sum(tot[rs, :], axis=1, keepdims=True), (tile, 128))
        return carry

    lax.fori_loop(0, nrow // tile, row_mass, 0)

    width = g_ref.shape[1]
    def turn(ci):
        return jnp.where(ci == 0, 2, jnp.where(ci == 1, 1, jnp.where(ci == 2, 3, 0)))

    def product(ci):
        q = lax.rem(y + turn(ci), NY)
        lanes = pl.ds(pl.multiple_of(q * width, width), width)
        moved = jnp.dot(plan_low[...], yg[:, lanes], preferred_element_type=jnp.float32)
        m = tot[...]
        for b in range(width // 128):
            cs = pl.ds(pl.multiple_of(q * width + b * 128, 128), 128)
            term[ci, :, b * 128 : (b + 1) * 128] = (
                xc[:, cs].astype(jnp.float32) * m - moved[:, b * 128 : (b + 1) * 128]
            )
        half_copy(ci).start()

    def half_copy(ci):
        return pltpu.make_async_remote_copy(
            term.at[ci, other_rows], half_in.at[ci], hs_sem.at[ci], hr_sem.at[ci],
            device_id=dev(dc=1), device_id_type=MESH,
        )

    def part_copy(ci):
        return pltpu.make_async_remote_copy(
            part_out.at[ci], part_in.at[ci], ps_sem.at[ci], pr_sem.at[ci],
            device_id=dev(dy=turn(ci)), device_id_type=MESH,
        )

    def pass_on(ci):
        half_copy(ci).wait()
        part_out[ci] = (term[ci, own_rows, :] + half_in[ci]).astype(jnp.bfloat16)
        part_copy(ci).start()

    def chunk(ci, carry):
        product(ci)

        @pl.when(ci > 0)
        def _():
            pass_on(ci - 1)

        @pl.when(ci == 2)
        def _():
            finish(lyr, 11)
            lzs[...] = lys[...] + sum(lyr[j] for j in range(len(y_peers)))
            start(lzs, lzr, 9, z_peers)

        return carry

    lax.fori_loop(0, NY, chunk, 0)
    half_copy(3).wait()
    term[3, own_rows, :] = term[3, own_rows, :] + half_in[3]
    finish(lzr, 9)
    lxs[...] = lzs[...] + sum(lzr[j] for j in range(len(z_peers)))
    start(lxs, lxr, 10, x_peers)
    part_copy(0).wait()
    part_copy(1).wait()
    term[3, own_rows, :] = (
        term[3, own_rows, :] + part_in[0].astype(jnp.float32) + part_in[1].astype(jnp.float32)
    )
    finish(lxr, 10)
    loss = lxs[...] + sum(lxr[j] for j in range(len(x_peers)))
    loss_ref[...] = jnp.broadcast_to(jnp.sum(loss, axis=1, keepdims=True) * (2.0 / depth), loss_ref.shape)
    part_copy(2).wait()
    g_ref[...] = float(new_total) * (term[3, own_rows, :] + part_in[2].astype(jnp.float32))
    others = (nz * NX - 1) * shard
    for i, part in ((0, "a"), (1, "b")):
        sent = yg.at[pl.ds(0, others), part_lanes[part]]
        pltpu.make_async_copy(sent, sent, gsend.at[i]).wait()


def solution(mesh):
    def body(new_embeddings, old_vectors):
        rows, depth = new_embeddings.shape
        shard = old_vectors.shape[0]
        nz = lax.axis_size("row") // (NX * NCORE)
        nrow, ncol = rows * NCORE, shard * nz * NX
        width = depth // NY
        f32, bf16 = jnp.float32, jnp.bfloat16
        ny, npx, npz = NY * NCORE - 1, NX - 1, nz - 1
        dma = pltpu.SemaphoreType.DMA
        scratch = [
            pltpu.VMEM((nrow, depth), bf16),
            pltpu.VMEM((ncol, depth), bf16),
            pltpu.VMEM((nrow, ncol), f32),
            pltpu.VMEM((nrow, ncol), f32),
            pltpu.VMEM((nrow, ncol), bf16),
            pltpu.VMEM((nrow, 128), f32),
            pltpu.VMEM((nrow, 128), f32),
            pltpu.VMEM((nrow, 128), f32),
            pltpu.VMEM((nrow, 128), f32),
            pltpu.VMEM((1, ncol), f32),
            pltpu.VMEM((1, ncol), f32),
            pltpu.VMEM((1, 2 * nrow), f32),
            pltpu.VMEM((ny, 1, 2 * nrow), f32),
            pltpu.VMEM((2, 1, nrow), f32),
            pltpu.VMEM((2, ny, 1, nrow), f32),
            pltpu.VMEM((1, 2 * ncol), f32),
            pltpu.VMEM((npx, 1, 2 * ncol), f32),
            pltpu.VMEM((1, 2 * ncol), f32),
            pltpu.VMEM((npz, 1, 2 * ncol), f32),
            pltpu.VMEM((2, 1, ncol), f32),
            pltpu.VMEM((2, npx, 1, ncol), f32),
            pltpu.VMEM((2, 1, ncol), f32),
            pltpu.VMEM((2, npz, 1, ncol), f32),
            pltpu.VMEM((1, 128), f32),
            pltpu.VMEM((npz, 1, 128), f32),
            pltpu.VMEM((1, 128), f32),
            pltpu.VMEM((npx, 1, 128), f32),
            pltpu.VMEM((1, 128), f32),
            pltpu.VMEM((ny, 1, 128), f32),
            pltpu.VMEM((4, nrow, width), f32),
            pltpu.VMEM((4, rows, width), f32),
            pltpu.VMEM((3, rows, width), bf16),
            pltpu.VMEM((3, rows, width), bf16),
            dma((2,)),
            dma((2,)),
            dma((2,)),
            dma((3,)),
            dma((2, nz // 2, 4)),
            dma((2, nz // 2)),
            dma((nz, 4)),
            dma((12,)),
            dma((12,)),
            dma((4,)),
            dma((4,)),
            dma((3,)),
            dma((3,)),
        ]
        gradient, loss = pl.pallas_call(
            body_kernel,
            out_shape=(
                pltpu.VMEM((rows, width), f32),
                pltpu.VMEM((1, 128), f32),
            ),
            in_specs=[pl.BlockSpec(memory_space=pl.ANY)] * 2,
            out_specs=[pl.BlockSpec(memory_space=pltpu.VMEM)] * 2,
            scratch_shapes=scratch,
            compiler_params=pltpu.CompilerParams(
                collective_id=0, has_side_effects=True, vmem_limit_bytes=56 << 20
            ),
            name="sinkhorn",
        )(new_embeddings, old_vectors)
        return gradient, loss[0, 0]

    placed = (P("row", None), P(("col", "row"), None))
    return jax.shard_map(
        body, mesh=mesh, in_specs=placed, out_specs=(P("row", "col"), P()), check_vma=False
    )
```

```python
import math

import jax
import jax.numpy as jnp
from jax import lax
from jax.experimental import pallas as pl
from jax.experimental.pallas import tpu as pltpu
from jax.sharding import PartitionSpec as P

MESH = pl.DeviceIdType.MESH
EPSILON = 0.01
RATE = 2.0 * math.log2(math.e) / EPSILON
LIFT = 40.0

NX, NCORE, NY = 4, 2, 4
SUB = 64


def body_kernel(
    x_hbm, y_hbm, g_ref, loss_ref,
    xc, yg, aff, ex, plan_low, xn, top, tot, rowb, vcol, tcol, loss_part,
    rs1, rr1, rs2, rr2,
    cxs1, cxr1, czs1, czr1, cxs2, cxr2, czs2, czr2,
    lzs, lzr, lxs, lxr, lys, lyr,
    term, half_in, part_out, part_in,
    local_sem, xcore_sem, gsend, ax_sem, az_sem, bz_sem, bx_sem,
    ex_send, ex_recv, hs_sem, hr_sem, ps_sem, pr_sem,
):
    rows, depth = x_hbm.shape
    shard = y_hbm.shape[0]
    nrow, ncol = aff.shape
    rate = RATE / depth
    nz = lax.axis_size("row") // (NX * NCORE)
    r = lax.axis_index("row")
    y = lax.axis_index("col")
    z = r // (NX * NCORE)
    x = (r // NCORE) % NX
    c = r % NCORE
    new_total = rows * lax.axis_size("row")
    old_total = shard * lax.axis_size("row") * lax.axis_size("col")
    lanes_a = 3 * depth // 8
    reach = nz // 2

    def dev(dz=0, dx=0, dc=0, dy=0):
        zz = lax.rem(z + dz + nz, nz)
        xx = lax.rem(x + dx + NX, NX)
        cc = lax.rem(c + dc, NCORE)
        yy = lax.rem(y + dy + NY, NY)
        return ((zz * NX + xx) * NCORE + cc, yy)

    z_peers = [dev(dz=d) for d in range(1, nz)]
    x_peers = [dev(dx=d) for d in range(1, NX)]
    y_peers = [dev(dy=d, dc=e) for d in range(NY) for e in range(NCORE) if d or e]

    barrier = pltpu.get_barrier_semaphore()
    everyone = z_peers + x_peers + y_peers
    for p in everyone:
        pl.semaphore_signal(barrier, inc=1, device_id=p, device_id_type=MESH)
    pl.semaphore_wait(barrier, len(everyone))

    part_lanes = {"a": pl.ds(0, lanes_a), "b": pl.ds(lanes_a, depth - lanes_a)}

    def region(dz, dx, part, half=None):
        slot = lax.rem(z + dz + nz, nz) * NX + lax.rem(x + dx + NX, NX)
        first = 0 if half is None else half * (shard // 2)
        count = shard if half is None else shard // 2
        start = pl.multiple_of(slot * shard + first, shard // 2)
        return yg.at[pl.ds(start, count), part_lanes[part]]

    def send(part, dst, sem, target, half=None, own=False):
        src = dst
        if own:
            src = y_hbm.at[:, part_lanes[part]]
        pltpu.make_async_remote_copy(
            src, dst, gsend.at[0 if part == "a" else 1], sem, device_id=target, device_id_type=MESH
        ).start()

    def arrived(ref, sem):
        pltpu.make_async_copy(ref, ref, sem).wait()

    zstep = (dev(dz=1), dev(dz=-1))
    zjump = (dev(dz=2), dev(dz=-2))
    xstep = (dev(dx=1), dev(dx=-1))
    xi_of = (0, -1, 1, 2)
    order_dz = [0] + [s * d for d in range(1, reach) for s in (-1, 1)] + [reach]
    place = {dz: i for i, dz in enumerate(order_dz)}

    def send_bx(dz, own=False):
        for way in (0, 1):
            send("b", region(dz, 0, "b"), bx_sem.at[place[dz], way], xstep[way], own=own)

    def send_az(xi, own=False):
        for way in (0, 1):
            send("a", region(0, xi_of[xi], "a"), az_sem.at[way, 0, xi], zstep[way], own=own)

    def on_ax(k):
        arrived(region(0, (-1, 1, 2)[k], "a"), ax_sem.at[k])
        send_az(1 + k)

    def on_az(way, d, xi):
        sign = -1 if way == 0 else 1
        here = region(sign * d, xi_of[xi], "a", None if d < reach else way)
        arrived(here, az_sem.at[way, d - 1, xi])
        if d < reach:
            half = None if d < reach - 1 else way
            send("a", region(sign * d, xi_of[xi], "a", half), az_sem.at[way, d, xi], zstep[way])

    def on_bz(way, d):
        sign = -1 if way == 0 else 1
        arrived(region(sign * d, 0, "b", None if d < reach else way), bz_sem.at[way, d - 1])
        if d == 2:
            send("b", region(sign * d, 0, "b"), bz_sem.at[way, 2], zstep[way])
            send("b", region(sign * d, 0, "b", way), bz_sem.at[way, 3], zjump[way])
        if d < reach:
            send_bx(sign * d)
        elif way == 1:
            send_bx(reach)

    def on_bx(dz, k):
        i = place[dz]
        if k < 2:
            dx = -1 if k == 0 else 1
            arrived(region(dz, dx, "b"), bx_sem.at[i, k])
            send("b", region(dz, dx, "b", k), bx_sem.at[i, 2 + k], xstep[k])
        else:
            arrived(region(dz, -2 if k == 2 else 2, "b", k - 2), bx_sem.at[i, k])

    own_slot = pl.ds(pl.multiple_of((z * NX + x) * shard, shard), shard)
    own_rows = pl.ds(pl.multiple_of(c * rows, rows), rows)
    other_rows = pl.ds(pl.multiple_of((1 - c) * rows, rows), rows)

    for way in (0, 1):
        send("b", region(0, 0, "b"), bz_sem.at[way, 0], zstep[way], own=True)
    for way in (0, 1):
        send("b", region(0, 0, "b"), bz_sem.at[way, 1], zjump[way], own=True)
    for k, target in enumerate((*xstep, dev(dx=2))):
        send("a", region(0, 0, "a"), ax_sem.at[k], target, own=True)
    send_az(0, own=True)
    send_bx(0, own=True)
    x_copy = pltpu.make_async_remote_copy(
        x_hbm, xc.at[own_rows], xcore_sem.at[0], xcore_sem.at[1], device_id=dev(dc=1), device_id_type=MESH
    )
    x_copy.start()
    x_local = pltpu.make_async_copy(x_hbm, xc.at[own_rows], local_sem.at[0])
    y_local = pltpu.make_async_copy(y_hbm, yg.at[own_slot], local_sem.at[1])
    x_local.start()
    y_local.start()

    top[...] = jnp.full(top.shape, -1e30, jnp.float32)
    tot[...] = jnp.zeros(tot.shape, jnp.float32)

    group = NX * shard
    tile = 256

    def compute(dz):
        col0 = pl.multiple_of(lax.rem(z + dz + nz, nz) * group, group)
        cols = pl.ds(col0, group)
        block = yg[cols, :]
        sq = jnp.square(block.astype(jnp.float32))
        part = sq[:, 0:128]
        for b in range(1, depth // 128):
            part = part + sq[:, b * 128 : (b + 1) * 128]
        half_norm = 0.5 * jnp.sum(jnp.transpose(part), axis=0, keepdims=True)
        inner = lax.dot_general(
            xc[...], block, (((1,), (1,)), ((), ())), preferred_element_type=jnp.float32
        )
        aff[:, cols] = inner - half_norm

        def step(i, carry):
            rs = pl.ds(pl.multiple_of(i * tile, tile), tile)
            best = top[rs, :]
            parts = [
                aff[rs, pl.ds(pl.multiple_of(col0 + b * 128, 128), 128)] for b in range(group // 128)
            ]
            high = best
            for val in parts:
                high = jnp.maximum(high, val)
            acc = tot[rs, :] * jnp.exp2((best - high) * rate)
            for val in parts:
                acc = acc + jnp.exp2((val - high) * rate)
            top[rs, :] = high
            tot[rs, :] = acc
            return carry

        lax.fori_loop(0, nrow // tile, step, 0)

    schedule = (
        (on_ax, 0), (on_ax, 1), (on_bz, 0, 1), (on_bz, 1, 1), (on_ax, 2), (on_bx, 0, 0), (on_bx, 0, 1),
        (on_bz, 0, 2), (on_bz, 1, 2), (on_az, 0, 1, 0), (on_az, 1, 1, 0), (on_bx, -1, 0), (on_bx, -1, 1),
        (on_az, 0, 1, 1), (on_az, 1, 1, 1), (on_bx, 1, 0), (on_bx, 1, 1), (on_az, 0, 1, 2), (on_az, 1, 1, 2),
        (on_bx, 0, 2), (on_bx, 0, 3), (compute, 0), (on_az, 0, 1, 3), (on_az, 1, 1, 3), (on_bx, -2, 0),
        (on_bx, -2, 1), (on_bz, 0, 3), (on_bz, 1, 3), (on_bx, 2, 0), (on_bx, 2, 1), (on_bz, 0, 4),
        (on_bz, 1, 4), (on_bx, -1, 2), (on_bx, -1, 3), (compute, -1), (on_az, 0, 2, 0), (on_az, 1, 2, 0),
        (on_bx, 1, 2), (on_bx, 1, 3), (compute, 1), (on_az, 0, 2, 1), (on_az, 1, 2, 1), (on_az, 0, 2, 2),
        (on_az, 1, 2, 2), (on_bx, -3, 0), (on_bx, -3, 1), (on_az, 0, 2, 3), (on_az, 1, 2, 3), (on_bx, -2, 2),
        (on_bx, -2, 3), (compute, -2), (on_az, 0, 3, 0), (on_bx, 3, 0), (on_az, 1, 3, 0), (on_bx, 3, 1),
        (on_bx, 2, 2), (on_bx, 2, 3), (compute, 2), (on_az, 0, 3, 1), (on_az, 1, 3, 1), (on_az, 0, 3, 2),
        (on_az, 1, 3, 2), (on_bx, 4, 0), (on_bx, 4, 1), (on_az, 0, 3, 3), (on_az, 1, 3, 3), (on_bx, -3, 2),
        (on_bx, -3, 3), (compute, -3), (on_bx, 3, 2), (on_bx, 3, 3), (compute, 3), (on_az, 0, 4, 0),
        (on_az, 1, 4, 0), (on_az, 0, 4, 1), (on_az, 1, 4, 1), (on_az, 0, 4, 2), (on_az, 1, 4, 2),
        (on_bx, 4, 2), (on_bx, 4, 3), (on_az, 0, 4, 3), (on_az, 1, 4, 3), (compute, 4),
    )
    stages = [[]]
    for act, *where in schedule:
        if act is compute:
            stages.append([])
        else:
            stages[-1].append((act, where))

    def stage(i, carry):
        for k, events in enumerate(stages[:nz]):

            @pl.when(i == k)
            def _(k=k, events=events):
                for act, where in events:
                    act(*where)
                if k == 0:
                    x_local.wait()
                    y_local.wait()
                    x_copy.wait()

        far = (i + 1) // 2
        compute(far - 2 * far * (i % 2))
        return carry

    lax.fori_loop(0, nz, stage, 0)

    def start(send_ref, recv_ref, i, peers):
        for j, p in enumerate(peers):
            pltpu.make_async_remote_copy(
                send_ref, recv_ref.at[j], ex_send.at[i], ex_recv.at[i], device_id=p, device_id_type=MESH
            ).start()

    def finish(recv_ref, i):
        pltpu.make_async_copy(recv_ref, recv_ref, ex_recv.at[i]).wait()
        pltpu.make_async_copy(recv_ref, recv_ref, ex_send.at[i]).wait()

    def to_rows(line):
        return jnp.transpose(jnp.broadcast_to(line, (128, nrow)))

    top_t = jnp.transpose(top[...])
    tot_t = jnp.transpose(tot[...])
    high = jnp.max(top_t, axis=0, keepdims=True)
    mass = jnp.sum(tot_t * jnp.exp2((top_t - high) * rate), axis=0, keepdims=True)
    rs1[:, 0:nrow] = high
    rs1[:, nrow : 2 * nrow] = mass
    start(rs1, rr1, 0, y_peers)

    def row_norms(i, carry):
        rs = pl.ds(pl.multiple_of(i * tile, tile), tile)
        part = jnp.zeros((tile, 128), jnp.float32)
        for b in range(depth // 128):
            part = part + jnp.square(xc[rs, b * 128 : (b + 1) * 128].astype(jnp.float32))
        xn[rs, :] = jnp.broadcast_to(0.5 * jnp.sum(part, axis=1, keepdims=True), (tile, 128))
        return carry

    lax.fori_loop(0, nrow // tile, row_norms, 0)
    finish(rr1, 0)
    highs = [high] + [rr1[j, :, 0:nrow] for j in range(len(y_peers))]
    masses = [mass] + [rr1[j, :, nrow : 2 * nrow] for j in range(len(y_peers))]
    high = highs[0]
    for v in highs[1:]:
        high = jnp.maximum(high, v)
    mass = sum(m * jnp.exp2((v - high) * rate) for v, m in zip(highs, masses))
    rowb[...] = to_rows(-high - (jnp.log2(mass) + math.log2(old_total)) / rate)

    nb = ncol // 128

    def fold(v, join):
        out = v[0:8]
        for i in range(1, v.shape[0] // 8):
            out = join(out, v[8 * i : 8 * i + 8])
        return out

    def highest(i, carry):
        rs = pl.ds(pl.multiple_of(i * SUB, SUB), SUB)
        rb = rowb[rs, :]
        out = []
        for b in range(nb):
            cs = pl.ds(b * 128, 128)
            a = rb + aff[rs, cs]
            ex[rs, cs] = a
            out.append(jnp.maximum(carry[b], fold(a, jnp.maximum)))
        return tuple(out)

    carry = lax.fori_loop(
        0, nrow // SUB, highest, tuple(jnp.full((8, 128), -3e38, jnp.float32) for _ in range(nb))
    )
    for b in range(nb):
        tcol[:, b * 128 : (b + 1) * 128] = jnp.max(carry[b], axis=0, keepdims=True) - LIFT / rate

    hb = nb // 2
    hc = ncol // 2
    spans = [range(h * hb, (h + 1) * hb) for h in range(2)]
    sides = [pl.ds(h * hc, hc) for h in range(2)]
    zeros = tuple(jnp.zeros((8, 128), jnp.float32) for _ in range(hb))

    def column_exchange(xs, xr, zs, zr, i, produce, merge, use):
        for h in range(2):
            produce(h)
            start(xs.at[h], xr.at[h], i + h, x_peers)
        for h in range(2):
            finish(xr.at[h], i + h)
            zs[h] = merge(xs, xr, h, len(x_peers))
            start(zs.at[h], zr.at[h], i + 2 + h, z_peers)
        for h in range(2):
            finish(zr.at[h], i + 2 + h)
            use(h, merge(zs, zr, h, len(z_peers)))

    def row_sums(h):
        def step(i, carry):
            rs = pl.ds(pl.multiple_of(i * SUB, SUB), SUB)
            acc = tot[rs, :] if h else None
            for b in spans[h]:
                cs = pl.ds(b * 128, 128)
                v = ex[rs, cs] * vcol[:, cs]
                acc = v if acc is None else acc + v
            tot[rs, :] = acc
            return carry

        lax.fori_loop(0, nrow // SUB, step, 0)

    grow = 2.0 ** (2 * LIFT) / new_total

    def scaled(h):
        def step(i, carry):
            rs = pl.ds(pl.multiple_of(i * SUB, SUB), SUB)
            out = []
            for n, b in enumerate(spans[h]):
                cs = pl.ds(b * 128, 128)
                e = jnp.exp2((ex[rs, cs] - tcol[:, cs]) * rate)
                ex[rs, cs] = e
                out.append(carry[n] + fold(e, jnp.add))
            return tuple(out)

        sums = lax.fori_loop(0, nrow // SUB, step, zeros)
        cxs1[h, :, 0:hc] = tcol[:, sides[h]]
        for n in range(hb):
            cxs1[h, :, hc + n * 128 : hc + (n + 1) * 128] = jnp.sum(sums[n], axis=0, keepdims=True)

    def merge_shifted(own, recv, h, n):
        tops = [own[h, :, 0:hc]] + [recv[h, j, :, 0:hc] for j in range(n)]
        sums = [own[h, :, hc:]] + [recv[h, j, :, hc:] for j in range(n)]
        best = tops[0]
        for v in tops[1:]:
            best = jnp.maximum(best, v)
        total = sum(t * jnp.exp2((v - best) * rate) for v, t in zip(tops, sums))
        return jnp.concatenate([best, total], axis=1)

    def first_factor(h, both):
        vcol[:, sides[h]] = jnp.exp2((tcol[:, sides[h]] - both[:, 0:hc]) * rate) * grow / both[:, hc:]
        row_sums(h)

    column_exchange(cxs1, cxr1, czs1, czr1, 1, scaled, merge_shifted, first_factor)

    loss_part[...] = jnp.zeros((8, 128), jnp.float32)

    def planned(h):
        def step(i, carry):
            rs = pl.ds(pl.multiple_of(i * SUB, SUB), SUB)
            rb = rowb[rs, :] * 2.0 ** (-2 * LIFT)
            xs = xn[rs, :]
            mass = tot[rs, :] if h else jnp.zeros((SUB, 128), jnp.float32)
            part = jnp.zeros((SUB, 128), jnp.float32)
            for b in spans[h]:
                cs = pl.ds(b * 128, 128)
                p = ex[rs, cs] * rb * vcol[:, cs]
                plan_low[rs, cs] = p.astype(jnp.bfloat16)
                mass = mass + p
                part = part + p * (xs - aff[rs, cs])
            tot[rs, :] = mass
            return carry + fold(part, jnp.add)

        loss_part[...] = lax.fori_loop(0, nrow // SUB, step, loss_part[...])

    def merge_sums(own, recv, h, n):
        return own[h] + sum(recv[h, j] for j in range(n))

    def again(sweep, carry):
        line = jnp.sum(jnp.transpose(tot[...]), axis=0, keepdims=True)
        i = 5 + 5 * sweep
        rs2[sweep] = line
        start(rs2.at[sweep], rr2.at[sweep], i, y_peers)
        finish(rr2.at[sweep], i)
        line = line + sum(rr2[sweep, j] for j in range(len(y_peers)))
        rowb[...] = to_rows((2.0 ** (2 * LIFT) / old_total) / line)

        def col_sums(h):
            def step(k, sums):
                rs = pl.ds(pl.multiple_of(k * SUB, SUB), SUB)
                rb = rowb[rs, :]
                return tuple(
                    sums[n] + fold(ex[rs, pl.ds(b * 128, 128)] * rb, jnp.add)
                    for n, b in enumerate(spans[h])
                )

            sums = lax.fori_loop(0, nrow // SUB, step, zeros)
            for n, b in enumerate(spans[h]):
                cxs2[sweep, h, :, n * 128 : (n + 1) * 128] = vcol[:, b * 128 : (b + 1) * 128] * jnp.sum(
                    sums[n], axis=0, keepdims=True
                )

        def next_factor(h, total):
            vcol[:, sides[h]] = vcol[:, sides[h]] * (grow / total)

            @pl.when(sweep == 0)
            def _():
                row_sums(h)

            @pl.when(sweep == 1)
            def _():
                planned(h)

        column_exchange(
            cxs2.at[sweep], cxr2.at[sweep], czs2.at[sweep], czr2.at[sweep], i + 1,
            col_sums, merge_sums, next_factor,
        )
        return carry

    lax.fori_loop(0, 2, again, 0)

    lys[...] = jnp.sum(loss_part[...], axis=0, keepdims=True)
    start(lys, lyr, 15, y_peers)

    def row_mass(i, carry):
        rs = pl.ds(pl.multiple_of(i * tile, tile), tile)
        tot[rs, :] = jnp.broadcast_to(jnp.sum(tot[rs, :], axis=1, keepdims=True), (tile, 128))
        return carry

    lax.fori_loop(0, nrow // tile, row_mass, 0)

    width = g_ref.shape[1]
    def turn(ci):
        return jnp.where(ci == 0, 2, jnp.where(ci == 1, 1, jnp.where(ci == 2, 3, 0)))

    def product(ci):
        q = lax.rem(y + turn(ci), NY)
        lanes = pl.ds(pl.multiple_of(q * width, width), width)
        moved = jnp.dot(plan_low[...], yg[:, lanes], preferred_element_type=jnp.float32)
        m = tot[...]
        for b in range(width // 128):
            cs = pl.ds(pl.multiple_of(q * width + b * 128, 128), 128)
            term[ci, :, b * 128 : (b + 1) * 128] = (
                xc[:, cs].astype(jnp.float32) * m - moved[:, b * 128 : (b + 1) * 128]
            )
        half_copy(ci).start()

    def half_copy(ci):
        return pltpu.make_async_remote_copy(
            term.at[ci, other_rows], half_in.at[ci], hs_sem.at[ci], hr_sem.at[ci],
            device_id=dev(dc=1), device_id_type=MESH,
        )

    def part_copy(ci):
        return pltpu.make_async_remote_copy(
            part_out.at[ci], part_in.at[ci], ps_sem.at[ci], pr_sem.at[ci],
            device_id=dev(dy=turn(ci)), device_id_type=MESH,
        )

    def pass_on(ci):
        half_copy(ci).wait()
        part_out[ci] = (term[ci, own_rows, :] + half_in[ci]).astype(jnp.bfloat16)
        part_copy(ci).start()

    def chunk(ci, carry):
        product(ci)

        @pl.when(ci > 0)
        def _():
            pass_on(ci - 1)

        @pl.when(ci == 2)
        def _():
            finish(lyr, 15)
            lzs[...] = lys[...] + sum(lyr[j] for j in range(len(y_peers)))
            start(lzs, lzr, 16, z_peers)

        return carry

    lax.fori_loop(0, NY, chunk, 0)
    half_copy(3).wait()
    term[3, own_rows, :] = term[3, own_rows, :] + half_in[3]
    finish(lzr, 16)
    lxs[...] = lzs[...] + sum(lzr[j] for j in range(len(z_peers)))
    start(lxs, lxr, 17, x_peers)
    part_copy(0).wait()
    part_copy(1).wait()
    term[3, own_rows, :] = (
        term[3, own_rows, :] + part_in[0].astype(jnp.float32) + part_in[1].astype(jnp.float32)
    )
    finish(lxr, 17)
    loss = lxs[...] + sum(lxr[j] for j in range(len(x_peers)))
    loss_ref[...] = jnp.broadcast_to(jnp.sum(loss, axis=1, keepdims=True) * (2.0 / depth), loss_ref.shape)
    part_copy(2).wait()
    g_ref[...] = float(new_total) * (term[3, own_rows, :] + part_in[2].astype(jnp.float32))
    others = (nz * NX - 1) * shard
    for i, part in ((0, "a"), (1, "b")):
        sent = yg.at[pl.ds(0, others), part_lanes[part]]
        pltpu.make_async_copy(sent, sent, gsend.at[i]).wait()


def solution(mesh):
    def body(new_embeddings, old_vectors):
        rows, depth = new_embeddings.shape
        shard = old_vectors.shape[0]
        nz = lax.axis_size("row") // (NX * NCORE)
        nrow, ncol = rows * NCORE, shard * nz * NX
        width = depth // NY
        f32, bf16 = jnp.float32, jnp.bfloat16
        ny, npx, npz = NY * NCORE - 1, NX - 1, nz - 1
        dma = pltpu.SemaphoreType.DMA
        scratch = [
            pltpu.VMEM((nrow, depth), bf16),
            pltpu.VMEM((ncol, depth), bf16),
            pltpu.VMEM((nrow, ncol), f32),
            pltpu.VMEM((nrow, ncol), f32),
            pltpu.VMEM((nrow, ncol), bf16),
            pltpu.VMEM((nrow, 128), f32),
            pltpu.VMEM((nrow, 128), f32),
            pltpu.VMEM((nrow, 128), f32),
            pltpu.VMEM((nrow, 128), f32),
            pltpu.VMEM((1, ncol), f32),
            pltpu.VMEM((1, ncol), f32),
            pltpu.VMEM((8, 128), f32),
            pltpu.VMEM((1, 2 * nrow), f32),
            pltpu.VMEM((ny, 1, 2 * nrow), f32),
            pltpu.VMEM((2, 1, nrow), f32),
            pltpu.VMEM((2, ny, 1, nrow), f32),
            pltpu.VMEM((2, 1, ncol), f32),
            pltpu.VMEM((2, npx, 1, ncol), f32),
            pltpu.VMEM((2, 1, ncol), f32),
            pltpu.VMEM((2, npz, 1, ncol), f32),
            pltpu.VMEM((2, 2, 1, ncol // 2), f32),
            pltpu.VMEM((2, 2, npx, 1, ncol // 2), f32),
            pltpu.VMEM((2, 2, 1, ncol // 2), f32),
            pltpu.VMEM((2, 2, npz, 1, ncol // 2), f32),
            pltpu.VMEM((1, 128), f32),
            pltpu.VMEM((npz, 1, 128), f32),
            pltpu.VMEM((1, 128), f32),
            pltpu.VMEM((npx, 1, 128), f32),
            pltpu.VMEM((1, 128), f32),
            pltpu.VMEM((ny, 1, 128), f32),
            pltpu.VMEM((4, nrow, width), f32),
            pltpu.VMEM((4, rows, width), f32),
            pltpu.VMEM((3, rows, width), bf16),
            pltpu.VMEM((3, rows, width), bf16),
            dma((2,)),
            dma((2,)),
            dma((2,)),
            dma((3,)),
            dma((2, nz // 2, 4)),
            dma((2, nz // 2)),
            dma((nz, 4)),
            dma((18,)),
            dma((18,)),
            dma((4,)),
            dma((4,)),
            dma((3,)),
            dma((3,)),
        ]
        gradient, loss = pl.pallas_call(
            body_kernel,
            out_shape=(
                pltpu.VMEM((rows, width), f32),
                pltpu.VMEM((1, 128), f32),
            ),
            in_specs=[pl.BlockSpec(memory_space=pl.ANY)] * 2,
            out_specs=[pl.BlockSpec(memory_space=pltpu.VMEM)] * 2,
            scratch_shapes=scratch,
            compiler_params=pltpu.CompilerParams(
                collective_id=0, has_side_effects=True, vmem_limit_bytes=56 << 20
            ),
            name="sinkhorn",
        )(new_embeddings, old_vectors)
        return gradient, loss[0, 0]

    placed = (P("row", None), P(("col", "row"), None))
    return jax.shard_map(
        body, mesh=mesh, in_specs=placed, out_specs=(P("row", "col"), P()), check_vma=False
    )
```

```python
import math

import jax
import jax.numpy as jnp
from jax import lax
from jax.experimental import pallas as pl
from jax.experimental.pallas import tpu as pltpu
from jax.sharding import PartitionSpec as P

MESH = pl.DeviceIdType.MESH
EPSILON = 0.01
RATE = 2.0 * math.log2(math.e) / EPSILON
LIFT = 40.0

NX, NCORE, NY = 4, 2, 4
SUB = 64


def body_kernel(
    x_hbm, y_hbm, g_ref, loss_ref,
    xc, yg, aff, ex, plan_low, xn, top, tot, rowb, vcol, tcol, loss_part,
    rs1, rr1, rs2, rr2,
    cxs1, cxr1, czs1, czr1, cxs2, cxr2, czs2, czr2,
    lzs, lzr, lxs, lxr, lys, lyr,
    term, half_in, part_out, part_in,
    local_sem, xcore_sem, gsend, ax_sem, az_sem, bz_sem, bx_sem,
    ex_send, ex_recv, hs_sem, hr_sem, ps_sem, pr_sem,
):
    rows, depth = x_hbm.shape
    shard = y_hbm.shape[0]
    nrow, ncol = aff.shape
    rate = RATE / depth
    nz = lax.axis_size("row") // (NX * NCORE)
    r = lax.axis_index("row")
    y = lax.axis_index("col")
    z = r // (NX * NCORE)
    x = (r // NCORE) % NX
    c = r % NCORE
    new_total = rows * lax.axis_size("row")
    old_total = shard * lax.axis_size("row") * lax.axis_size("col")
    lanes_a = 3 * depth // 8
    reach = nz // 2

    def dev(dz=0, dx=0, dc=0, dy=0):
        zz = lax.rem(z + dz + nz, nz)
        xx = lax.rem(x + dx + NX, NX)
        cc = lax.rem(c + dc, NCORE)
        yy = lax.rem(y + dy + NY, NY)
        return ((zz * NX + xx) * NCORE + cc, yy)

    z_peers = [dev(dz=d) for d in range(1, nz)]
    x_peers = [dev(dx=d) for d in range(1, NX)]
    y_peers = [dev(dy=d, dc=e) for d in range(NY) for e in range(NCORE) if d or e]

    barrier = pltpu.get_barrier_semaphore()
    everyone = z_peers + x_peers + y_peers
    for p in everyone:
        pl.semaphore_signal(barrier, inc=1, device_id=p, device_id_type=MESH)
    pl.semaphore_wait(barrier, len(everyone))

    part_lanes = {"a": pl.ds(0, lanes_a), "b": pl.ds(lanes_a, depth - lanes_a)}

    def region(dz, dx, part, half=None):
        slot = lax.rem(z + dz + nz, nz) * NX + lax.rem(x + dx + NX, NX)
        first = 0 if half is None else half * (shard // 2)
        count = shard if half is None else shard // 2
        start = pl.multiple_of(slot * shard + first, shard // 2)
        return yg.at[pl.ds(start, count), part_lanes[part]]

    def send(part, dst, sem, target, half=None, own=False):
        src = dst
        if own:
            src = y_hbm.at[:, part_lanes[part]]
        pltpu.make_async_remote_copy(
            src, dst, gsend.at[0 if part == "a" else 1], sem, device_id=target, device_id_type=MESH
        ).start()

    def arrived(ref, sem):
        pltpu.make_async_copy(ref, ref, sem).wait()

    zstep = (dev(dz=1), dev(dz=-1))
    zjump = (dev(dz=2), dev(dz=-2))
    xstep = (dev(dx=1), dev(dx=-1))
    xi_of = (0, -1, 1, 2)
    order_dz = [0] + [s * d for d in range(1, reach) for s in (-1, 1)] + [reach]
    place = {dz: i for i, dz in enumerate(order_dz)}

    def send_bx(dz, own=False):
        for way in (0, 1):
            send("b", region(dz, 0, "b"), bx_sem.at[place[dz], way], xstep[way], own=own)

    def send_az(xi, own=False):
        for way in (0, 1):
            send("a", region(0, xi_of[xi], "a"), az_sem.at[way, 0, xi], zstep[way], own=own)

    def on_ax(k):
        arrived(region(0, (-1, 1, 2)[k], "a"), ax_sem.at[k])
        send_az(1 + k)

    def on_az(way, d, xi):
        sign = -1 if way == 0 else 1
        here = region(sign * d, xi_of[xi], "a", None if d < reach else way)
        arrived(here, az_sem.at[way, d - 1, xi])
        if d < reach:
            half = None if d < reach - 1 else way
            send("a", region(sign * d, xi_of[xi], "a", half), az_sem.at[way, d, xi], zstep[way])

    def on_bz(way, d):
        sign = -1 if way == 0 else 1
        arrived(region(sign * d, 0, "b", None if d < reach else way), bz_sem.at[way, d - 1])
        if d == 2:
            send("b", region(sign * d, 0, "b"), bz_sem.at[way, 2], zstep[way])
            send("b", region(sign * d, 0, "b", way), bz_sem.at[way, 3], zjump[way])
        if d < reach:
            send_bx(sign * d)
        elif way == 1:
            send_bx(reach)

    def on_bx(dz, k):
        i = place[dz]
        if k < 2:
            dx = -1 if k == 0 else 1
            arrived(region(dz, dx, "b"), bx_sem.at[i, k])
            send("b", region(dz, dx, "b", k), bx_sem.at[i, 2 + k], xstep[k])
        else:
            arrived(region(dz, -2 if k == 2 else 2, "b", k - 2), bx_sem.at[i, k])

    own_slot = pl.ds(pl.multiple_of((z * NX + x) * shard, shard), shard)
    own_rows = pl.ds(pl.multiple_of(c * rows, rows), rows)
    other_rows = pl.ds(pl.multiple_of((1 - c) * rows, rows), rows)

    for way in (0, 1):
        send("b", region(0, 0, "b"), bz_sem.at[way, 0], zstep[way], own=True)
    for k, target in enumerate((*xstep, dev(dx=2))):
        send("a", region(0, 0, "a"), ax_sem.at[k], target, own=True)
    for way in (0, 1):
        send("b", region(0, 0, "b"), bz_sem.at[way, 1], zjump[way], own=True)
    send_bx(0, own=True)
    send_az(0, own=True)
    x_copy = pltpu.make_async_remote_copy(
        x_hbm, xc.at[own_rows], xcore_sem.at[0], xcore_sem.at[1], device_id=dev(dc=1), device_id_type=MESH
    )
    x_copy.start()
    x_local = pltpu.make_async_copy(x_hbm, xc.at[own_rows], local_sem.at[0])
    y_local = pltpu.make_async_copy(y_hbm, yg.at[own_slot], local_sem.at[1])
    x_local.start()
    y_local.start()

    top[...] = jnp.full(top.shape, -1e30, jnp.float32)
    tot[...] = jnp.zeros(tot.shape, jnp.float32)

    group = NX * shard
    tile = 256

    def compute(dz):
        col0 = pl.multiple_of(lax.rem(z + dz + nz, nz) * group, group)
        cols = pl.ds(col0, group)
        block = yg[cols, :]
        sq = jnp.square(block.astype(jnp.float32))
        part = sq[:, 0:128]
        for b in range(1, depth // 128):
            part = part + sq[:, b * 128 : (b + 1) * 128]
        half_norm = 0.5 * jnp.sum(jnp.transpose(part), axis=0, keepdims=True)
        inner = lax.dot_general(
            xc[...], block, (((1,), (1,)), ((), ())), preferred_element_type=jnp.float32
        )
        aff[:, cols] = inner - half_norm

        def step(i, carry):
            rs = pl.ds(pl.multiple_of(i * tile, tile), tile)
            best = top[rs, :]
            parts = [
                aff[rs, pl.ds(pl.multiple_of(col0 + b * 128, 128), 128)] for b in range(group // 128)
            ]
            high = best
            for val in parts:
                high = jnp.maximum(high, val)
            acc = tot[rs, :] * jnp.exp2((best - high) * rate)
            for val in parts:
                acc = acc + jnp.exp2((val - high) * rate)
            top[rs, :] = high
            tot[rs, :] = acc
            return carry

        lax.fori_loop(0, nrow // tile, step, 0)

    schedule = (
        (on_ax, 0), (on_ax, 1), (on_bz, 0, 1), (on_bz, 1, 1), (on_ax, 2), (on_bx, 0, 0), (on_bx, 0, 1),
        (on_bz, 0, 2), (on_bz, 1, 2), (on_az, 0, 1, 0), (on_az, 1, 1, 0), (on_bx, -1, 0), (on_bx, -1, 1),
        (on_az, 0, 1, 1), (on_az, 1, 1, 1), (on_bx, 1, 0), (on_bx, 1, 1), (on_az, 0, 1, 2), (on_az, 1, 1, 2),
        (on_bx, 0, 2), (on_bx, 0, 3), (compute, 0), (on_az, 0, 1, 3), (on_az, 1, 1, 3), (on_bx, -2, 0),
        (on_bx, -2, 1), (on_bz, 0, 3), (on_bz, 1, 3), (on_bx, 2, 0), (on_bx, 2, 1), (on_bz, 0, 4),
        (on_bz, 1, 4), (on_bx, -1, 2), (on_bx, -1, 3), (compute, -1), (on_az, 0, 2, 0), (on_az, 1, 2, 0),
        (on_bx, 1, 2), (on_bx, 1, 3), (compute, 1), (on_az, 0, 2, 1), (on_az, 1, 2, 1), (on_az, 0, 2, 2),
        (on_az, 1, 2, 2), (on_bx, -3, 0), (on_bx, -3, 1), (on_az, 0, 2, 3), (on_az, 1, 2, 3), (on_bx, -2, 2),
        (on_bx, -2, 3), (compute, -2), (on_az, 0, 3, 0), (on_bx, 3, 0), (on_az, 1, 3, 0), (on_bx, 3, 1),
        (on_bx, 2, 2), (on_bx, 2, 3), (compute, 2), (on_az, 0, 3, 1), (on_az, 1, 3, 1), (on_az, 0, 3, 2),
        (on_az, 1, 3, 2), (on_bx, 4, 0), (on_bx, 4, 1), (on_az, 0, 3, 3), (on_az, 1, 3, 3), (on_bx, -3, 2),
        (on_bx, -3, 3), (compute, -3), (on_bx, 3, 2), (on_bx, 3, 3), (compute, 3), (on_az, 0, 4, 0),
        (on_az, 1, 4, 0), (on_az, 0, 4, 1), (on_az, 1, 4, 1), (on_az, 0, 4, 2), (on_az, 1, 4, 2),
        (on_bx, 4, 2), (on_bx, 4, 3), (on_az, 0, 4, 3), (on_az, 1, 4, 3), (compute, 4),
    )
    stages = [[]]
    for act, *where in schedule:
        if act is compute:
            stages.append([])
        else:
            stages[-1].append((act, where))

    def stage(i, carry):
        for k, events in enumerate(stages[:nz]):

            @pl.when(i == k)
            def _(k=k, events=events):
                for act, where in events:
                    act(*where)
                if k == 0:
                    x_local.wait()
                    y_local.wait()
                    x_copy.wait()

        far = (i + 1) // 2
        compute(far - 2 * far * (i % 2))
        return carry

    lax.fori_loop(0, nz, stage, 0)

    def start(send_ref, recv_ref, i, peers):
        for j, p in enumerate(peers):
            pltpu.make_async_remote_copy(
                send_ref, recv_ref.at[j], ex_send.at[i], ex_recv.at[i], device_id=p, device_id_type=MESH
            ).start()

    def finish(recv_ref, i):
        pltpu.make_async_copy(recv_ref, recv_ref, ex_recv.at[i]).wait()
        pltpu.make_async_copy(recv_ref, recv_ref, ex_send.at[i]).wait()

    def to_rows(line):
        return jnp.transpose(jnp.broadcast_to(line, (128, nrow)))

    top_t = jnp.transpose(top[...])
    tot_t = jnp.transpose(tot[...])
    high = jnp.max(top_t, axis=0, keepdims=True)
    mass = jnp.sum(tot_t * jnp.exp2((top_t - high) * rate), axis=0, keepdims=True)
    rs1[:, 0:nrow] = high
    rs1[:, nrow : 2 * nrow] = mass
    start(rs1, rr1, 0, y_peers)

    def row_norms(i, carry):
        rs = pl.ds(pl.multiple_of(i * tile, tile), tile)
        part = jnp.zeros((tile, 128), jnp.float32)
        for b in range(depth // 128):
            part = part + jnp.square(xc[rs, b * 128 : (b + 1) * 128].astype(jnp.float32))
        xn[rs, :] = jnp.broadcast_to(0.5 * jnp.sum(part, axis=1, keepdims=True), (tile, 128))
        return carry

    lax.fori_loop(0, nrow // tile, row_norms, 0)
    finish(rr1, 0)
    highs = [high] + [rr1[j, :, 0:nrow] for j in range(len(y_peers))]
    masses = [mass] + [rr1[j, :, nrow : 2 * nrow] for j in range(len(y_peers))]
    high = highs[0]
    for v in highs[1:]:
        high = jnp.maximum(high, v)
    mass = sum(m * jnp.exp2((v - high) * rate) for v, m in zip(highs, masses))
    rowb[...] = to_rows(-high - (jnp.log2(mass) + math.log2(old_total)) / rate)

    nb = ncol // 128

    def fold(v, join):
        out = v[0:8]
        for i in range(1, v.shape[0] // 8):
            out = join(out, v[8 * i : 8 * i + 8])
        return out

    def highest(i, carry):
        rs = pl.ds(pl.multiple_of(i * SUB, SUB), SUB)
        rb = rowb[rs, :]
        out = []
        for b in range(nb):
            cs = pl.ds(b * 128, 128)
            a = rb + aff[rs, cs]
            ex[rs, cs] = a
            out.append(jnp.maximum(carry[b], fold(a, jnp.maximum)))
        return tuple(out)

    carry = lax.fori_loop(
        0, nrow // SUB, highest, tuple(jnp.full((8, 128), -3e38, jnp.float32) for _ in range(nb))
    )
    for b in range(nb):
        tcol[:, b * 128 : (b + 1) * 128] = jnp.max(carry[b], axis=0, keepdims=True) - LIFT / rate

    hb = nb // 2
    hc = ncol // 2
    spans = [range(h * hb, (h + 1) * hb) for h in range(2)]
    sides = [pl.ds(h * hc, hc) for h in range(2)]
    zeros = tuple(jnp.zeros((8, 128), jnp.float32) for _ in range(hb))

    def column_exchange(xs, xr, zs, zr, i, produce, merge, use):
        for h in range(2):
            produce(h)
            start(xs.at[h], xr.at[h], i + h, x_peers)
        for h in range(2):
            finish(xr.at[h], i + h)
            zs[h] = merge(xs, xr, h, len(x_peers))
            start(zs.at[h], zr.at[h], i + 2 + h, z_peers)
        for h in range(2):
            finish(zr.at[h], i + 2 + h)
            use(h, merge(zs, zr, h, len(z_peers)))

    def row_sums(h):
        def step(i, carry):
            rs = pl.ds(pl.multiple_of(i * SUB, SUB), SUB)
            acc = tot[rs, :] if h else None
            for b in spans[h]:
                cs = pl.ds(b * 128, 128)
                v = ex[rs, cs] * vcol[:, cs]
                acc = v if acc is None else acc + v
            tot[rs, :] = acc
            return carry

        lax.fori_loop(0, nrow // SUB, step, 0)

    grow = 2.0 ** (2 * LIFT) / new_total

    def scaled(h):
        def step(i, carry):
            rs = pl.ds(pl.multiple_of(i * SUB, SUB), SUB)
            out = []
            for n, b in enumerate(spans[h]):
                cs = pl.ds(b * 128, 128)
                e = jnp.exp2((ex[rs, cs] - tcol[:, cs]) * rate)
                ex[rs, cs] = e
                out.append(carry[n] + fold(e, jnp.add))
            return tuple(out)

        sums = lax.fori_loop(0, nrow // SUB, step, zeros)
        cxs1[h, :, 0:hc] = tcol[:, sides[h]]
        for n in range(hb):
            cxs1[h, :, hc + n * 128 : hc + (n + 1) * 128] = jnp.sum(sums[n], axis=0, keepdims=True)

    def merge_shifted(own, recv, h, n):
        tops = [own[h, :, 0:hc]] + [recv[h, j, :, 0:hc] for j in range(n)]
        sums = [own[h, :, hc:]] + [recv[h, j, :, hc:] for j in range(n)]
        best = tops[0]
        for v in tops[1:]:
            best = jnp.maximum(best, v)
        total = sum(t * jnp.exp2((v - best) * rate) for v, t in zip(tops, sums))
        return jnp.concatenate([best, total], axis=1)

    def first_factor(h, both):
        vcol[:, sides[h]] = jnp.exp2((tcol[:, sides[h]] - both[:, 0:hc]) * rate) * grow / both[:, hc:]
        row_sums(h)

    column_exchange(cxs1, cxr1, czs1, czr1, 1, scaled, merge_shifted, first_factor)

    loss_part[...] = jnp.zeros((8, 128), jnp.float32)

    def planned(h):
        def step(i, carry):
            rs = pl.ds(pl.multiple_of(i * SUB, SUB), SUB)
            rb = rowb[rs, :] * 2.0 ** (-2 * LIFT)
            xs = xn[rs, :]
            mass = tot[rs, :] if h else jnp.zeros((SUB, 128), jnp.float32)
            part = jnp.zeros((SUB, 128), jnp.float32)
            for b in spans[h]:
                cs = pl.ds(b * 128, 128)
                p = ex[rs, cs] * rb * vcol[:, cs]
                plan_low[rs, cs] = p.astype(jnp.bfloat16)
                mass = mass + p
                part = part + p * (xs - aff[rs, cs])
            tot[rs, :] = mass
            return carry + fold(part, jnp.add)

        loss_part[...] = lax.fori_loop(0, nrow // SUB, step, loss_part[...])

    def merge_sums(own, recv, h, n):
        return own[h] + sum(recv[h, j] for j in range(n))

    def again(sweep, carry):
        line = jnp.sum(jnp.transpose(tot[...]), axis=0, keepdims=True)
        i = 5 + 5 * sweep
        rs2[sweep] = line
        start(rs2.at[sweep], rr2.at[sweep], i, y_peers)
        finish(rr2.at[sweep], i)
        line = line + sum(rr2[sweep, j] for j in range(len(y_peers)))
        rowb[...] = to_rows((2.0 ** (2 * LIFT) / old_total) / line)

        def col_sums(h):
            def step(k, sums):
                rs = pl.ds(pl.multiple_of(k * SUB, SUB), SUB)
                rb = rowb[rs, :]
                return tuple(
                    sums[n] + fold(ex[rs, pl.ds(b * 128, 128)] * rb, jnp.add)
                    for n, b in enumerate(spans[h])
                )

            sums = lax.fori_loop(0, nrow // SUB, step, zeros)
            for n, b in enumerate(spans[h]):
                cxs2[sweep, h, :, n * 128 : (n + 1) * 128] = vcol[:, b * 128 : (b + 1) * 128] * jnp.sum(
                    sums[n], axis=0, keepdims=True
                )

        def next_factor(h, total):
            vcol[:, sides[h]] = vcol[:, sides[h]] * (grow / total)

            @pl.when(sweep == 0)
            def _():
                row_sums(h)

            @pl.when(sweep == 1)
            def _():
                planned(h)

        column_exchange(
            cxs2.at[sweep], cxr2.at[sweep], czs2.at[sweep], czr2.at[sweep], i + 1,
            col_sums, merge_sums, next_factor,
        )
        return carry

    lax.fori_loop(0, 2, again, 0)

    lys[...] = jnp.sum(loss_part[...], axis=0, keepdims=True)
    start(lys, lyr, 15, y_peers)

    def row_mass(i, carry):
        rs = pl.ds(pl.multiple_of(i * tile, tile), tile)
        tot[rs, :] = jnp.broadcast_to(jnp.sum(tot[rs, :], axis=1, keepdims=True), (tile, 128))
        return carry

    lax.fori_loop(0, nrow // tile, row_mass, 0)

    width = g_ref.shape[1]
    def turn(ci):
        return jnp.where(ci == 0, 2, jnp.where(ci == 1, 1, jnp.where(ci == 2, 3, 0)))

    def product(ci):
        q = lax.rem(y + turn(ci), NY)
        lanes = pl.ds(pl.multiple_of(q * width, width), width)
        moved = jnp.dot(plan_low[...], yg[:, lanes], preferred_element_type=jnp.float32)
        m = tot[...]
        for b in range(width // 128):
            cs = pl.ds(pl.multiple_of(q * width + b * 128, 128), 128)
            term[ci, :, b * 128 : (b + 1) * 128] = (
                xc[:, cs].astype(jnp.float32) * m - moved[:, b * 128 : (b + 1) * 128]
            )
        half_copy(ci).start()

    def half_copy(ci):
        return pltpu.make_async_remote_copy(
            term.at[ci, other_rows], half_in.at[ci], hs_sem.at[ci], hr_sem.at[ci],
            device_id=dev(dc=1), device_id_type=MESH,
        )

    def part_copy(ci):
        return pltpu.make_async_remote_copy(
            part_out.at[ci], part_in.at[ci], ps_sem.at[ci], pr_sem.at[ci],
            device_id=dev(dy=turn(ci)), device_id_type=MESH,
        )

    def pass_on(ci):
        half_copy(ci).wait()
        part_out[ci] = (term[ci, own_rows, :] + half_in[ci]).astype(jnp.bfloat16)
        part_copy(ci).start()

    def chunk(ci, carry):
        product(ci)

        @pl.when(ci > 0)
        def _():
            pass_on(ci - 1)

        @pl.when(ci == 2)
        def _():
            finish(lyr, 15)
            lzs[...] = lys[...] + sum(lyr[j] for j in range(len(y_peers)))
            start(lzs, lzr, 16, z_peers)

        return carry

    lax.fori_loop(0, NY, chunk, 0)
    half_copy(3).wait()
    term[3, own_rows, :] = term[3, own_rows, :] + half_in[3]
    finish(lzr, 16)
    lxs[...] = lzs[...] + sum(lzr[j] for j in range(len(z_peers)))
    start(lxs, lxr, 17, x_peers)
    part_copy(0).wait()
    part_copy(1).wait()
    term[3, own_rows, :] = (
        term[3, own_rows, :] + part_in[0].astype(jnp.float32) + part_in[1].astype(jnp.float32)
    )
    finish(lxr, 17)
    loss = lxs[...] + sum(lxr[j] for j in range(len(x_peers)))
    loss_ref[...] = jnp.broadcast_to(jnp.sum(loss, axis=1, keepdims=True) * (2.0 / depth), loss_ref.shape)
    part_copy(2).wait()
    g_ref[...] = float(new_total) * (term[3, own_rows, :] + part_in[2].astype(jnp.float32))
    others = (nz * NX - 1) * shard
    for i, part in ((0, "a"), (1, "b")):
        sent = yg.at[pl.ds(0, others), part_lanes[part]]
        pltpu.make_async_copy(sent, sent, gsend.at[i]).wait()


def solution(mesh):
    def body(new_embeddings, old_vectors):
        rows, depth = new_embeddings.shape
        shard = old_vectors.shape[0]
        nz = lax.axis_size("row") // (NX * NCORE)
        nrow, ncol = rows * NCORE, shard * nz * NX
        width = depth // NY
        f32, bf16 = jnp.float32, jnp.bfloat16
        ny, npx, npz = NY * NCORE - 1, NX - 1, nz - 1
        dma = pltpu.SemaphoreType.DMA
        scratch = [
            pltpu.VMEM((nrow, depth), bf16),
            pltpu.VMEM((ncol, depth), bf16),
            pltpu.VMEM((nrow, ncol), f32),
            pltpu.VMEM((nrow, ncol), f32),
            pltpu.VMEM((nrow, ncol), bf16),
            pltpu.VMEM((nrow, 128), f32),
            pltpu.VMEM((nrow, 128), f32),
            pltpu.VMEM((nrow, 128), f32),
            pltpu.VMEM((nrow, 128), f32),
            pltpu.VMEM((1, ncol), f32),
            pltpu.VMEM((1, ncol), f32),
            pltpu.VMEM((8, 128), f32),
            pltpu.VMEM((1, 2 * nrow), f32),
            pltpu.VMEM((ny, 1, 2 * nrow), f32),
            pltpu.VMEM((2, 1, nrow), f32),
            pltpu.VMEM((2, ny, 1, nrow), f32),
            pltpu.VMEM((2, 1, ncol), f32),
            pltpu.VMEM((2, npx, 1, ncol), f32),
            pltpu.VMEM((2, 1, ncol), f32),
            pltpu.VMEM((2, npz, 1, ncol), f32),
            pltpu.VMEM((2, 2, 1, ncol // 2), f32),
            pltpu.VMEM((2, 2, npx, 1, ncol // 2), f32),
            pltpu.VMEM((2, 2, 1, ncol // 2), f32),
            pltpu.VMEM((2, 2, npz, 1, ncol // 2), f32),
            pltpu.VMEM((1, 128), f32),
            pltpu.VMEM((npz, 1, 128), f32),
            pltpu.VMEM((1, 128), f32),
            pltpu.VMEM((npx, 1, 128), f32),
            pltpu.VMEM((1, 128), f32),
            pltpu.VMEM((ny, 1, 128), f32),
            pltpu.VMEM((4, nrow, width), f32),
            pltpu.VMEM((4, rows, width), f32),
            pltpu.VMEM((3, rows, width), bf16),
            pltpu.VMEM((3, rows, width), bf16),
            dma((2,)),
            dma((2,)),
            dma((2,)),
            dma((3,)),
            dma((2, nz // 2, 4)),
            dma((2, nz // 2)),
            dma((nz, 4)),
            dma((18,)),
            dma((18,)),
            dma((4,)),
            dma((4,)),
            dma((3,)),
            dma((3,)),
        ]
        gradient, loss = pl.pallas_call(
            body_kernel,
            out_shape=(
                pltpu.VMEM((rows, width), f32),
                pltpu.VMEM((1, 128), f32),
            ),
            in_specs=[pl.BlockSpec(memory_space=pl.ANY)] * 2,
            out_specs=[pl.BlockSpec(memory_space=pltpu.VMEM)] * 2,
            scratch_shapes=scratch,
            compiler_params=pltpu.CompilerParams(
                collective_id=0, has_side_effects=True, vmem_limit_bytes=56 << 20
            ),
            name="sinkhorn",
        )(new_embeddings, old_vectors)
        return gradient, loss[0, 0]

    placed = (P("row", None), P(("col", "row"), None))
    return jax.shard_map(
        body, mesh=mesh, in_specs=placed, out_specs=(P("row", "col"), P()), check_vma=False
    )
```

```python
import math

import jax
import jax.numpy as jnp
from jax import lax
from jax.experimental import pallas as pl
from jax.experimental.pallas import tpu as pltpu
from jax.sharding import PartitionSpec as P

MESH = pl.DeviceIdType.MESH
EPSILON = 0.01
RATE = 2.0 * math.log2(math.e) / EPSILON
LIFT = 40.0

NX, NCORE, NY = 4, 2, 4
SUB = 64


def body_kernel(
    x_hbm, y_hbm, g_ref, loss_ref,
    xc, yg, aff, ex, plan_low, xn, top, tot, rowb, vcol, tcol, loss_part,
    rs1, rr1, rs2, rr2,
    cxs1, cxr1, czs1, czr1, cxs2, cxr2, czs2, czr2,
    lzs, lzr, lxs, lxr, lys, lyr,
    term, half_in, part_out, part_in,
    local_sem, xcore_sem, gsend, ax_sem, az_sem, bz_sem, bx_sem,
    ex_send, ex_recv, hs_sem, hr_sem, ps_sem, pr_sem,
):
    rows, depth = x_hbm.shape
    shard = y_hbm.shape[0]
    nrow, ncol = aff.shape
    rate = RATE / depth
    nz = lax.axis_size("row") // (NX * NCORE)
    r = lax.axis_index("row")
    y = lax.axis_index("col")
    z = r // (NX * NCORE)
    x = (r // NCORE) % NX
    c = r % NCORE
    new_total = rows * lax.axis_size("row")
    old_total = shard * lax.axis_size("row") * lax.axis_size("col")
    lanes_a = 3 * depth // 8
    reach = nz // 2

    def dev(dz=0, dx=0, dc=0, dy=0):
        zz = lax.rem(z + dz + nz, nz)
        xx = lax.rem(x + dx + NX, NX)
        cc = lax.rem(c + dc, NCORE)
        yy = lax.rem(y + dy + NY, NY)
        return ((zz * NX + xx) * NCORE + cc, yy)

    z_peers = [dev(dz=d) for d in range(1, nz)]
    x_peers = [dev(dx=d) for d in range(1, NX)]
    y_peers = [dev(dy=d, dc=e) for d in range(NY) for e in range(NCORE) if d or e]

    barrier = pltpu.get_barrier_semaphore()
    everyone = z_peers + x_peers + y_peers
    for p in everyone:
        pl.semaphore_signal(barrier, inc=1, device_id=p, device_id_type=MESH)
    pl.semaphore_wait(barrier, len(everyone))

    part_lanes = {"a": pl.ds(0, lanes_a), "b": pl.ds(lanes_a, depth - lanes_a)}

    def region(dz, dx, part, half=None):
        slot = lax.rem(z + dz + nz, nz) * NX + lax.rem(x + dx + NX, NX)
        first = 0 if half is None else half * (shard // 2)
        count = shard if half is None else shard // 2
        start = pl.multiple_of(slot * shard + first, shard // 2)
        return yg.at[pl.ds(start, count), part_lanes[part]]

    def send(part, dst, sem, target, half=None, own=False):
        src = dst
        if own:
            src = y_hbm.at[:, part_lanes[part]]
        pltpu.make_async_remote_copy(
            src, dst, gsend.at[0 if part == "a" else 1], sem, device_id=target, device_id_type=MESH
        ).start()

    def arrived(ref, sem):
        pltpu.make_async_copy(ref, ref, sem).wait()

    zstep = (dev(dz=1), dev(dz=-1))
    zjump = (dev(dz=2), dev(dz=-2))
    xstep = (dev(dx=1), dev(dx=-1))
    xi_of = (0, -1, 1, 2)
    order_dz = [0] + [s * d for d in range(1, reach) for s in (-1, 1)] + [reach]
    place = {dz: i for i, dz in enumerate(order_dz)}

    def send_bx(dz, own=False):
        for way in (0, 1):
            send("b", region(dz, 0, "b"), bx_sem.at[place[dz], way], xstep[way], own=own)

    def send_az(xi, own=False):
        for way in (0, 1):
            send("a", region(0, xi_of[xi], "a"), az_sem.at[way, 0, xi], zstep[way], own=own)

    def on_ax(k):
        arrived(region(0, (-1, 1, 2)[k], "a"), ax_sem.at[k])
        send_az(1 + k)

    def on_az(way, d, xi):
        sign = -1 if way == 0 else 1
        here = region(sign * d, xi_of[xi], "a", None if d < reach else way)
        arrived(here, az_sem.at[way, d - 1, xi])
        if d < reach:
            half = None if d < reach - 1 else way
            send("a", region(sign * d, xi_of[xi], "a", half), az_sem.at[way, d, xi], zstep[way])

    def on_bz(way, d):
        sign = -1 if way == 0 else 1
        arrived(region(sign * d, 0, "b", None if d < reach else way), bz_sem.at[way, d - 1])
        if d == 2:
            send("b", region(sign * d, 0, "b"), bz_sem.at[way, 2], zstep[way])
            send("b", region(sign * d, 0, "b", way), bz_sem.at[way, 3], zjump[way])
        if d < reach:
            send_bx(sign * d)
        elif way == 1:
            send_bx(reach)

    def on_bx(dz, k):
        i = place[dz]
        if k < 2:
            dx = -1 if k == 0 else 1
            arrived(region(dz, dx, "b"), bx_sem.at[i, k])
            send("b", region(dz, dx, "b", k), bx_sem.at[i, 2 + k], xstep[k])
        else:
            arrived(region(dz, -2 if k == 2 else 2, "b", k - 2), bx_sem.at[i, k])

    own_slot = pl.ds(pl.multiple_of((z * NX + x) * shard, shard), shard)
    own_rows = pl.ds(pl.multiple_of(c * rows, rows), rows)
    other_rows = pl.ds(pl.multiple_of((1 - c) * rows, rows), rows)

    for way in (0, 1):
        send("b", region(0, 0, "b"), bz_sem.at[way, 0], zstep[way], own=True)
    for k, target in enumerate((*xstep, dev(dx=2))):
        send("a", region(0, 0, "a"), ax_sem.at[k], target, own=True)
    for way in (0, 1):
        send("b", region(0, 0, "b"), bz_sem.at[way, 1], zjump[way], own=True)
    send_bx(0, own=True)
    send_az(0, own=True)
    x_copy = pltpu.make_async_remote_copy(
        x_hbm, xc.at[own_rows], xcore_sem.at[0], xcore_sem.at[1], device_id=dev(dc=1), device_id_type=MESH
    )
    x_copy.start()
    x_local = pltpu.make_async_copy(x_hbm, xc.at[own_rows], local_sem.at[0])
    y_local = pltpu.make_async_copy(y_hbm, yg.at[own_slot], local_sem.at[1])
    x_local.start()
    y_local.start()

    top[...] = jnp.full(top.shape, -1e30, jnp.float32)
    tot[...] = jnp.zeros(tot.shape, jnp.float32)

    group = NX * shard
    tile = 256

    def compute(dz):
        col0 = pl.multiple_of(lax.rem(z + dz + nz, nz) * group, group)
        cols = pl.ds(col0, group)
        block = yg[cols, :]
        sq = jnp.square(block.astype(jnp.float32))
        part = sq[:, 0:128]
        for b in range(1, depth // 128):
            part = part + sq[:, b * 128 : (b + 1) * 128]
        half_norm = 0.5 * jnp.sum(jnp.transpose(part), axis=0, keepdims=True)
        inner = lax.dot_general(
            xc[...], block, (((1,), (1,)), ((), ())), preferred_element_type=jnp.float32
        )
        aff[:, cols] = inner - half_norm

        def step(i, carry):
            rs = pl.ds(pl.multiple_of(i * tile, tile), tile)
            best = top[rs, :]
            parts = [
                aff[rs, pl.ds(pl.multiple_of(col0 + b * 128, 128), 128)] for b in range(group // 128)
            ]
            high = best
            for val in parts:
                high = jnp.maximum(high, val)
            acc = tot[rs, :] * jnp.exp2((best - high) * rate)
            for val in parts:
                acc = acc + jnp.exp2((val - high) * rate)
            top[rs, :] = high
            tot[rs, :] = acc
            return carry

        lax.fori_loop(0, nrow // tile, step, 0)

    schedule = (
        (on_ax, 0), (on_ax, 1), (on_bz, 0, 1), (on_bz, 1, 1), (on_ax, 2), (on_bx, 0, 0), (on_bx, 0, 1),
        (on_bz, 0, 2), (on_bz, 1, 2), (on_az, 0, 1, 0), (on_az, 1, 1, 0), (on_bx, -1, 0), (on_bx, -1, 1),
        (on_az, 0, 1, 1), (on_az, 1, 1, 1), (on_bx, 1, 0), (on_bx, 1, 1), (on_az, 0, 1, 2), (on_az, 1, 1, 2),
        (on_bx, 0, 2), (on_bx, 0, 3), (compute, 0), (on_az, 0, 1, 3), (on_az, 1, 1, 3), (on_bx, -2, 0),
        (on_bx, -2, 1), (on_bz, 0, 3), (on_bz, 1, 3), (on_bx, 2, 0), (on_bx, 2, 1), (on_bz, 0, 4),
        (on_bz, 1, 4), (on_bx, -1, 2), (on_bx, -1, 3), (compute, -1), (on_az, 0, 2, 0), (on_az, 1, 2, 0),
        (on_bx, 1, 2), (on_bx, 1, 3), (compute, 1), (on_az, 0, 2, 1), (on_az, 1, 2, 1), (on_az, 0, 2, 2),
        (on_az, 1, 2, 2), (on_bx, -3, 0), (on_bx, -3, 1), (on_az, 0, 2, 3), (on_az, 1, 2, 3), (on_bx, -2, 2),
        (on_bx, -2, 3), (compute, -2), (on_az, 0, 3, 0), (on_bx, 3, 0), (on_az, 1, 3, 0), (on_bx, 3, 1),
        (on_bx, 2, 2), (on_bx, 2, 3), (compute, 2), (on_az, 0, 3, 1), (on_az, 1, 3, 1), (on_az, 0, 3, 2),
        (on_az, 1, 3, 2), (on_bx, 4, 0), (on_bx, 4, 1), (on_az, 0, 3, 3), (on_az, 1, 3, 3), (on_bx, -3, 2),
        (on_bx, -3, 3), (compute, -3), (on_bx, 3, 2), (on_bx, 3, 3), (compute, 3), (on_az, 0, 4, 0),
        (on_az, 1, 4, 0), (on_az, 0, 4, 1), (on_az, 1, 4, 1), (on_az, 0, 4, 2), (on_az, 1, 4, 2),
        (on_bx, 4, 2), (on_bx, 4, 3), (on_az, 0, 4, 3), (on_az, 1, 4, 3), (compute, 4),
    )
    stages = [[]]
    for act, *where in schedule:
        if act is compute:
            stages.append([])
        else:
            stages[-1].append((act, where))

    def stage(i, carry):
        for k, events in enumerate(stages[:nz]):

            @pl.when(i == k)
            def _(k=k, events=events):
                for act, where in events:
                    act(*where)
                if k == 0:
                    x_local.wait()
                    y_local.wait()
                    x_copy.wait()

        far = (i + 1) // 2
        compute(far - 2 * far * (i % 2))
        return carry

    lax.fori_loop(0, nz, stage, 0)

    def start(send_ref, recv_ref, i, peers):
        for j, p in enumerate(peers):
            pltpu.make_async_remote_copy(
                send_ref, recv_ref.at[j], ex_send.at[i], ex_recv.at[i], device_id=p, device_id_type=MESH
            ).start()

    def finish(recv_ref, i):
        pltpu.make_async_copy(recv_ref, recv_ref, ex_recv.at[i]).wait()
        pltpu.make_async_copy(recv_ref, recv_ref, ex_send.at[i]).wait()

    def to_rows(line):
        return jnp.transpose(jnp.broadcast_to(line, (128, nrow)))

    top_t = jnp.transpose(top[...])
    tot_t = jnp.transpose(tot[...])
    high = jnp.max(top_t, axis=0, keepdims=True)
    mass = jnp.sum(tot_t * jnp.exp2((top_t - high) * rate), axis=0, keepdims=True)
    rs1[:, 0:nrow] = high
    rs1[:, nrow : 2 * nrow] = mass
    start(rs1, rr1, 0, y_peers)

    def row_norms(i, carry):
        rs = pl.ds(pl.multiple_of(i * tile, tile), tile)
        part = jnp.zeros((tile, 128), jnp.float32)
        for b in range(depth // 128):
            part = part + jnp.square(xc[rs, b * 128 : (b + 1) * 128].astype(jnp.float32))
        xn[rs, :] = jnp.broadcast_to(0.5 * jnp.sum(part, axis=1, keepdims=True), (tile, 128))
        return carry

    lax.fori_loop(0, nrow // tile, row_norms, 0)
    finish(rr1, 0)
    highs = [high] + [rr1[j, :, 0:nrow] for j in range(len(y_peers))]
    masses = [mass] + [rr1[j, :, nrow : 2 * nrow] for j in range(len(y_peers))]
    high = highs[0]
    for v in highs[1:]:
        high = jnp.maximum(high, v)
    mass = sum(m * jnp.exp2((v - high) * rate) for v, m in zip(highs, masses))
    rowb[...] = to_rows(-high - (jnp.log2(mass) + math.log2(old_total)) / rate)

    nb = ncol // 128

    def fold(v, join):
        out = v[0:8]
        for i in range(1, v.shape[0] // 8):
            out = join(out, v[8 * i : 8 * i + 8])
        return out

    def highest(i, carry):
        rs = pl.ds(pl.multiple_of(i * SUB, SUB), SUB)
        rb = rowb[rs, :]
        out = []
        for b in range(nb):
            cs = pl.ds(b * 128, 128)
            a = rb + aff[rs, cs]
            ex[rs, cs] = a
            out.append(jnp.maximum(carry[b], fold(a, jnp.maximum)))
        return tuple(out)

    carry = lax.fori_loop(
        0, nrow // SUB, highest, tuple(jnp.full((8, 128), -3e38, jnp.float32) for _ in range(nb))
    )
    for b in range(nb):
        tcol[:, b * 128 : (b + 1) * 128] = jnp.max(carry[b], axis=0, keepdims=True) - LIFT / rate

    hb = nb // 2
    hc = ncol // 2
    spans = [range(h * hb, (h + 1) * hb) for h in range(2)]
    sides = [pl.ds(h * hc, hc) for h in range(2)]
    zeros = tuple(jnp.zeros((8, 128), jnp.float32) for _ in range(hb))

    def column_exchange(xs, xr, zs, zr, i, produce, merge, use):
        for h in range(2):
            produce(h)
            start(xs.at[h], xr.at[h], i + h, x_peers)
        for h in range(2):
            finish(xr.at[h], i + h)
            zs[h] = merge(xs, xr, h, len(x_peers))
            start(zs.at[h], zr.at[h], i + 2 + h, z_peers)
        for h in range(2):
            finish(zr.at[h], i + 2 + h)
            use(h, merge(zs, zr, h, len(z_peers)))

    def row_sums(h):
        def step(i, carry):
            rs = pl.ds(pl.multiple_of(i * SUB, SUB), SUB)
            acc = tot[rs, :] if h else None
            for b in spans[h]:
                cs = pl.ds(b * 128, 128)
                v = ex[rs, cs] * vcol[:, cs]
                acc = v if acc is None else acc + v
            tot[rs, :] = acc
            return carry

        lax.fori_loop(0, nrow // SUB, step, 0)

    grow = 2.0 ** (2 * LIFT) / new_total

    def scaled(h):
        def step(i, carry):
            rs = pl.ds(pl.multiple_of(i * SUB, SUB), SUB)
            out = []
            for n, b in enumerate(spans[h]):
                cs = pl.ds(b * 128, 128)
                e = jnp.exp2((ex[rs, cs] - tcol[:, cs]) * rate)
                ex[rs, cs] = e
                out.append(carry[n] + fold(e, jnp.add))
            return tuple(out)

        sums = lax.fori_loop(0, nrow // SUB, step, zeros)
        cxs1[h, :, 0:hc] = tcol[:, sides[h]]
        for n in range(hb):
            cxs1[h, :, hc + n * 128 : hc + (n + 1) * 128] = jnp.sum(sums[n], axis=0, keepdims=True)

    def merge_shifted(own, recv, h, n):
        tops = [own[h, :, 0:hc]] + [recv[h, j, :, 0:hc] for j in range(n)]
        sums = [own[h, :, hc:]] + [recv[h, j, :, hc:] for j in range(n)]
        best = tops[0]
        for v in tops[1:]:
            best = jnp.maximum(best, v)
        total = sum(t * jnp.exp2((v - best) * rate) for v, t in zip(tops, sums))
        return jnp.concatenate([best, total], axis=1)

    def first_factor(h, both):
        vcol[:, sides[h]] = jnp.exp2((tcol[:, sides[h]] - both[:, 0:hc]) * rate) * grow / both[:, hc:]
        row_sums(h)

    column_exchange(cxs1, cxr1, czs1, czr1, 1, scaled, merge_shifted, first_factor)

    loss_part[...] = jnp.zeros((8, 128), jnp.float32)

    def planned(h):
        def step(i, carry):
            rs = pl.ds(pl.multiple_of(i * SUB, SUB), SUB)
            rb = rowb[rs, :] * 2.0 ** (-2 * LIFT)
            xs = xn[rs, :]
            mass = tot[rs, :] if h else jnp.zeros((SUB, 128), jnp.float32)
            part = jnp.zeros((SUB, 128), jnp.float32)
            for b in spans[h]:
                cs = pl.ds(b * 128, 128)
                p = ex[rs, cs] * rb * vcol[:, cs]
                plan_low[rs, cs] = p.astype(jnp.bfloat16)
                mass = mass + p
                part = part + p * (xs - aff[rs, cs])
            tot[rs, :] = mass
            return carry + fold(part, jnp.add)

        loss_part[...] = lax.fori_loop(0, nrow // SUB, step, loss_part[...])

    def merge_sums(own, recv, h, n):
        return own[h] + sum(recv[h, j] for j in range(n))

    def again(sweep, carry):
        line = jnp.sum(jnp.transpose(tot[...]), axis=0, keepdims=True)
        i = 5 + 5 * sweep
        rs2[sweep] = line
        start(rs2.at[sweep], rr2.at[sweep], i, y_peers)
        finish(rr2.at[sweep], i)
        line = line + sum(rr2[sweep, j] for j in range(len(y_peers)))
        rowb[...] = to_rows((2.0 ** (2 * LIFT) / old_total) / line)

        def col_sums(h):
            def step(k, sums):
                rs = pl.ds(pl.multiple_of(k * SUB, SUB), SUB)
                rb = rowb[rs, :]
                return tuple(
                    sums[n] + fold(ex[rs, pl.ds(b * 128, 128)] * rb, jnp.add)
                    for n, b in enumerate(spans[h])
                )

            sums = lax.fori_loop(0, nrow // SUB, step, zeros)
            for n, b in enumerate(spans[h]):
                cxs2[sweep, h, :, n * 128 : (n + 1) * 128] = vcol[:, b * 128 : (b + 1) * 128] * jnp.sum(
                    sums[n], axis=0, keepdims=True
                )

        def next_factor(h, total):
            vcol[:, sides[h]] = vcol[:, sides[h]] * (grow / total)

            @pl.when(sweep == 0)
            def _():
                row_sums(h)

            @pl.when(sweep == 1)
            def _():
                planned(h)

        column_exchange(
            cxs2.at[sweep], cxr2.at[sweep], czs2.at[sweep], czr2.at[sweep], i + 1,
            col_sums, merge_sums, next_factor,
        )
        return carry

    lax.fori_loop(0, 2, again, 0)

    lys[...] = jnp.sum(loss_part[...], axis=0, keepdims=True)
    start(lys, lyr, 15, y_peers)

    def row_mass(i, carry):
        rs = pl.ds(pl.multiple_of(i * tile, tile), tile)
        tot[rs, :] = jnp.broadcast_to(jnp.sum(tot[rs, :], axis=1, keepdims=True), (tile, 128))
        return carry

    lax.fori_loop(0, nrow // tile, row_mass, 0)

    width = g_ref.shape[1]
    def turn(ci):
        return jnp.where(ci == 0, 1, jnp.where(ci == 1, 3, jnp.where(ci == 2, 2, 0)))

    def product(ci):
        q = lax.rem(y + turn(ci), NY)
        lanes = pl.ds(pl.multiple_of(q * width, width), width)
        moved = jnp.dot(plan_low[...], yg[:, lanes], preferred_element_type=jnp.float32)
        m = tot[...]
        for b in range(width // 128):
            cs = pl.ds(pl.multiple_of(q * width + b * 128, 128), 128)
            term[ci, :, b * 128 : (b + 1) * 128] = (
                xc[:, cs].astype(jnp.float32) * m - moved[:, b * 128 : (b + 1) * 128]
            )
        half_copy(ci).start()

    def half_copy(ci):
        return pltpu.make_async_remote_copy(
            term.at[ci, other_rows], half_in.at[ci], hs_sem.at[ci], hr_sem.at[ci],
            device_id=dev(dc=1), device_id_type=MESH,
        )

    def part_copy(ci):
        return pltpu.make_async_remote_copy(
            part_out.at[ci], part_in.at[ci], ps_sem.at[ci], pr_sem.at[ci],
            device_id=dev(dy=turn(ci)), device_id_type=MESH,
        )

    def pass_on(ci):
        half_copy(ci).wait()
        part_out[ci] = (term[ci, own_rows, :] + half_in[ci]).astype(jnp.bfloat16)
        part_copy(ci).start()

    def chunk(ci, carry):
        product(ci)

        @pl.when(ci > 0)
        def _():
            pass_on(ci - 1)

        @pl.when(ci == 2)
        def _():
            finish(lyr, 15)
            lzs[...] = lys[...] + sum(lyr[j] for j in range(len(y_peers)))
            start(lzs, lzr, 16, z_peers)

        return carry

    lax.fori_loop(0, NY, chunk, 0)
    half_copy(3).wait()
    term[3, own_rows, :] = term[3, own_rows, :] + half_in[3]
    finish(lzr, 16)
    lxs[...] = lzs[...] + sum(lzr[j] for j in range(len(z_peers)))
    start(lxs, lxr, 17, x_peers)
    part_copy(0).wait()
    part_copy(1).wait()
    term[3, own_rows, :] = (
        term[3, own_rows, :] + part_in[0].astype(jnp.float32) + part_in[1].astype(jnp.float32)
    )
    finish(lxr, 17)
    loss = lxs[...] + sum(lxr[j] for j in range(len(x_peers)))
    loss_ref[...] = jnp.broadcast_to(jnp.sum(loss, axis=1, keepdims=True) * (2.0 / depth), loss_ref.shape)
    part_copy(2).wait()
    g_ref[...] = float(new_total) * (term[3, own_rows, :] + part_in[2].astype(jnp.float32))
    others = (nz * NX - 1) * shard
    for i, part in ((0, "a"), (1, "b")):
        sent = yg.at[pl.ds(0, others), part_lanes[part]]
        pltpu.make_async_copy(sent, sent, gsend.at[i]).wait()


def solution(mesh):
    def body(new_embeddings, old_vectors):
        rows, depth = new_embeddings.shape
        shard = old_vectors.shape[0]
        nz = lax.axis_size("row") // (NX * NCORE)
        nrow, ncol = rows * NCORE, shard * nz * NX
        width = depth // NY
        f32, bf16 = jnp.float32, jnp.bfloat16
        ny, npx, npz = NY * NCORE - 1, NX - 1, nz - 1
        dma = pltpu.SemaphoreType.DMA
        scratch = [
            pltpu.VMEM((nrow, depth), bf16),
            pltpu.VMEM((ncol, depth), bf16),
            pltpu.VMEM((nrow, ncol), f32),
            pltpu.VMEM((nrow, ncol), f32),
            pltpu.VMEM((nrow, ncol), bf16),
            pltpu.VMEM((nrow, 128), f32),
            pltpu.VMEM((nrow, 128), f32),
            pltpu.VMEM((nrow, 128), f32),
            pltpu.VMEM((nrow, 128), f32),
            pltpu.VMEM((1, ncol), f32),
            pltpu.VMEM((1, ncol), f32),
            pltpu.VMEM((8, 128), f32),
            pltpu.VMEM((1, 2 * nrow), f32),
            pltpu.VMEM((ny, 1, 2 * nrow), f32),
            pltpu.VMEM((2, 1, nrow), f32),
            pltpu.VMEM((2, ny, 1, nrow), f32),
            pltpu.VMEM((2, 1, ncol), f32),
            pltpu.VMEM((2, npx, 1, ncol), f32),
            pltpu.VMEM((2, 1, ncol), f32),
            pltpu.VMEM((2, npz, 1, ncol), f32),
            pltpu.VMEM((2, 2, 1, ncol // 2), f32),
            pltpu.VMEM((2, 2, npx, 1, ncol // 2), f32),
            pltpu.VMEM((2, 2, 1, ncol // 2), f32),
            pltpu.VMEM((2, 2, npz, 1, ncol // 2), f32),
            pltpu.VMEM((1, 128), f32),
            pltpu.VMEM((npz, 1, 128), f32),
            pltpu.VMEM((1, 128), f32),
            pltpu.VMEM((npx, 1, 128), f32),
            pltpu.VMEM((1, 128), f32),
            pltpu.VMEM((ny, 1, 128), f32),
            pltpu.VMEM((4, nrow, width), f32),
            pltpu.VMEM((4, rows, width), f32),
            pltpu.VMEM((3, rows, width), bf16),
            pltpu.VMEM((3, rows, width), bf16),
            dma((2,)),
            dma((2,)),
            dma((2,)),
            dma((3,)),
            dma((2, nz // 2, 4)),
            dma((2, nz // 2)),
            dma((nz, 4)),
            dma((18,)),
            dma((18,)),
            dma((4,)),
            dma((4,)),
            dma((3,)),
            dma((3,)),
        ]
        gradient, loss = pl.pallas_call(
            body_kernel,
            out_shape=(
                pltpu.VMEM((rows, width), f32),
                pltpu.VMEM((1, 128), f32),
            ),
            in_specs=[pl.BlockSpec(memory_space=pl.ANY)] * 2,
            out_specs=[pl.BlockSpec(memory_space=pltpu.VMEM)] * 2,
            scratch_shapes=scratch,
            compiler_params=pltpu.CompilerParams(
                collective_id=0, has_side_effects=True, vmem_limit_bytes=56 << 20
            ),
            name="sinkhorn",
        )(new_embeddings, old_vectors)
        return gradient, loss[0, 0]

    placed = (P("row", None), P(("col", "row"), None))
    return jax.shard_map(
        body, mesh=mesh, in_specs=placed, out_specs=(P("row", "col"), P()), check_vma=False
    )
```
